512 devices in a mesh: band: 32 (over x_lo, y, core), ga: 16 (over x_hi, z).
Axes of the slice: x: 4 (x_hi: 2, x_lo: 2; x = x_hi * 2 + x_lo), y: 8, z: 8, core: 2. Of those that a mesh axis runs over, the one named last changes fastest.
Arguments:
- orbitals: float32 [32, 2, 128, 4096], P('band', None, None, 'ga'), may hold values from -6 to 6
- orbital_tangent: float32 [32, 2, 128, 4096], P('band', None, None, 'ga'), may hold values from -6 to 6
- stick_columns: int32 [4096], replicated, may hold values from 0 to 16383, as said below
- ion_potential: float32 [128, 128, 128], P('ga'), may hold values from -6 to 6
- core_density: float32 [128, 128, 128], P('ga'), may hold values from 0.5 to 2
- positions: float32 [2000, 3], replicated, may hold values from 0 to 40
- z_charge: float32 [2000], replicated, may hold values from 2 to 8
- widths: float32 [2000], replicated, may hold values from 1.5 to 4
- atom_index: int32 [8], replicated, may hold values from 0 to 1999
- direction: int32 [8], replicated, may hold values from 0 to 2
Outputs:
- hessian_product: float32 [32, 2, 128, 4096], P('band', None, None, 'ga')
The draws below stay inside these ranges and needn't reach their ends.
Inputs may be any that keep to these rules, and one draw needn't show every extreme that they name: `stick_columns`: 4096 distinct columns gx * 128 + gy, among them every column whose signed frequencies satisfy sx^2 + sy^2 <= 32^2, in no particular order.
All inputs are finite; a program needn't handle non-finite values.
Results may differ from the reference program's by a relative error of at most 0.0001.
Values sent between devices are 32-bit elements; how exact they have to be, the bound alone decides.
No kernel may reach another device: no remote copies, remote signals or barrier semaphores. Data moves between devices by JAX's collectives and lax.ppermute only.
A program may use at most 128 MiB of HBM per device.

```python
import math
import jax
import jax.numpy as jnp
from jax import lax

N = 128
ATOMS = 2000
DISP = 8
BANDS = 32
STICKS = 4096


def draw_stick_columns(key, part):
    key = jax.random.fold_in(key, 7)
    first_key, second_key = jax.random.split(key)
    every = jnp.arange(N * N, dtype=jnp.int32)
    across = every // N
    inplane = every % N
    across = jnp.where(across >= N // 2, across - N, across)
    inplane = jnp.where(inplane >= N // 2, inplane - N, inplane)
    inside = across * across + inplane * inplane <= (N // 4) ** 2
    noise = jax.random.randint(first_key, (N * N,), 0, N * N)
    score = jnp.where(inside, N * N, noise) * (N * N) + every
    chosen = lax.top_k(score, STICKS)[1]
    order = jax.random.permutation(second_key, STICKS)
    return chosen[order].astype(jnp.int32)


def place_ends(entries, own_key, smallest, largest):
    shape = entries.shape
    index_at = [jax.random.randint(jax.random.fold_in(own_key, axis), (), 0, shape[axis]) for axis in range(len(shape))]
    entries = entries.at[tuple(index_at)].set(smallest)
    longest = shape.index(max(shape))
    index_at[longest] = (index_at[longest] + 1) % shape[longest]
    return entries.at[tuple(index_at)].set(largest)


def shard_levels(own_key, shape, cuts, least, top_value):
    def one(dim, parts):
        steps = jax.random.uniform(jax.random.fold_in(jax.random.fold_in(own_key, 6), dim), (parts,), jnp.float32, least / len(cuts), top_value / len(cuts))
        return jnp.repeat(jnp.exp(steps), shape[dim] // parts).reshape((-1,) + (1,) * (len(shape) - dim - 1))

    loudness = one(*cuts[0])
    for cut in cuts[1:]:
        loudness = loudness * one(*cut)
    return loudness


def normal_values(own_key, dims, deviation, bound, cuts=(), kind=jnp.bfloat16):
    entries = jax.random.normal(own_key, dims, jnp.float32) * deviation
    if len(cuts) > 0:
        entries = shard_levels(own_key, dims, cuts, -0.22, 0.18) * entries
    return jnp.clip(entries, min=-bound, max=bound).astype(kind)


def setup_inputs(seed: int = 0) -> dict:
    keys = jax.random.split(jax.random.key(seed), 11)
    orbitals = normal_values(keys[0], (BANDS, 2, N, STICKS), 1.0, 6.0, ((0, 32), (3, 16)), jnp.float32)
    orbital_tangent = normal_values(keys[1], (BANDS, 2, N, STICKS), 1.0, 6.0, ((0, 32), (3, 16)), jnp.float32)
    stick_columns = draw_stick_columns(jax.random.fold_in(keys[10], 71), 0)
    ion_potential = normal_values(keys[3], (N, N, N), 1.0, 6.0, ((0, 16),), jnp.float32)
    core_density = jnp.clip(jnp.exp(math.log(2.0) - 1.3862944 * jax.random.uniform(keys[4], (N, N, N), jnp.float32) ** shard_levels(keys[4], (N, N, N), ((0, 16),), -0.2, 0.2)), 0.5, 2.0)
    positions = jnp.clip(jax.random.uniform(keys[5], (ATOMS, 3), jnp.float32, 0.0, 40.0), 0.0, 40.0)
    z_charge = jnp.clip(jnp.exp(jax.random.uniform(keys[6], (ATOMS,), jnp.float32, math.log(2.0), math.log(8.0))), 2.0, 8.0)
    widths = jnp.clip(jnp.exp(jax.random.uniform(keys[7], (ATOMS,), jnp.float32, math.log(1.5), math.log(4.0))), 1.5, 4.0)
    atom_index = place_ends(jax.random.randint(keys[8], (DISP,), 0, ATOMS), jax.random.fold_in(keys[8], 1), 0, ATOMS - 1).astype(jnp.int32)
    direction = place_ends(jax.random.randint(keys[9], (DISP,), 0, 3), jax.random.fold_in(keys[9], 1), 0, 2).astype(jnp.int32)
    return {"orbitals": orbitals, "orbital_tangent": orbital_tangent, "stick_columns": stick_columns, "ion_potential": ion_potential, "core_density": core_density, "positions": positions, "z_charge": z_charge, "widths": widths, "atom_index": atom_index, "direction": direction}


cell_length = 40.0
slater_factor = (3.0 / math.pi) ** (1.0 / 3.0)


def signed_freq(values, length):
    return jnp.where(values >= length // 2, values - length, values)


def ion_profile(length, centre, spread, axis_id, chosen):
    frequency = signed_freq(jnp.arange(length, dtype=jnp.int32), length).astype(jnp.float32)
    wavenum = frequency * (2.0 * math.pi / cell_length)
    coords = jnp.arange(length, dtype=jnp.float32) * (cell_length / length)
    damping = jnp.exp(-0.5 * (wavenum * spread) ** 2)
    phases = wavenum[:, None] * (coords[None, :] - centre)
    smooth = jnp.sum(damping[:, None] * jnp.cos(phases), 0)
    slope = jnp.sum((damping * wavenum)[:, None] * jnp.sin(phases), 0)
    return jnp.where(chosen == axis_id, slope, smooth)


def reference(orbitals, orbital_tangent, stick_columns, ion_potential, core_density, positions, z_charge, widths, atom_index, direction):
    weight = 4.0 / N ** 1.5
    frequency = signed_freq(jnp.arange(N, dtype=jnp.int32), N)
    across = signed_freq(stick_columns // N, N)
    inplane = signed_freq(stick_columns % N, N)
    radius = (frequency * frequency)[:, None] + (across * across + inplane * inplane)[None, :]
    sphere = (radius <= (N // 4) ** 2).astype(jnp.float32)

    def real_field(coefficients):
        masked = coefficients * sphere
        empty = jnp.zeros((N, N * N), jnp.float32)
        boxed = lax.complex(empty, empty).at[:, stick_columns].set(lax.complex(masked[0], masked[1]))
        return jnp.fft.ifftn(boxed.reshape(N, N, N)) * (weight * N ** 3)

    def accumulate(carry, couple):
        first = real_field(couple[0])
        second = real_field(couple[1])
        dens_sum = carry[0] + jnp.real(first) ** 2 + jnp.imag(first) ** 2
        resp_sum = carry[1] + jnp.real(first) * jnp.real(second) + jnp.imag(first) * jnp.imag(second)
        return (dens_sum, resp_sum), None

    zero_field = jnp.zeros((N, N, N), jnp.float32)
    sums, ignored = lax.scan(accumulate, (zero_field, zero_field), (orbitals, orbital_tangent))
    density = sums[0] / BANDS
    response = 2.0 * sums[1] / BANDS

    total = density + core_density
    exchange_potential = -slater_factor * total ** (1.0 / 3.0)
    exchange_kernel = -(slater_factor / 3.0) * total ** (-2.0 / 3.0)

    every = jnp.arange(N * N, dtype=jnp.int32)
    col_across = signed_freq(every // N, N)
    col_inplane = signed_freq(every % N, N)
    squares = (frequency * frequency)[:, None] + (col_across * col_across + col_inplane * col_inplane)[None, :]
    nonzero = jnp.where(squares == 0, 1, squares).astype(jnp.float32)
    factor = (2.0 * math.pi / cell_length) ** 2
    kernel = jnp.where(squares == 0, 0.0, 4.0 * math.pi / (factor * nonzero)).reshape(N, N, N)
    hartree = jnp.real(jnp.fft.ifftn(jnp.fft.fftn(response) * kernel))

    ion_change = jnp.zeros((N, N, N), jnp.float32)
    for slot in range(DISP):
        chosen_atom = atom_index[slot]
        axis_pick = direction[slot]
        charge = z_charge[chosen_atom]
        spread = widths[chosen_atom]
        centre = positions[chosen_atom]
        along_x = ion_profile(N, centre[0], spread, 0, axis_pick)
        along_y = ion_profile(N, centre[1], spread, 1, axis_pick)
        along_z = ion_profile(N, centre[2], spread, 2, axis_pick)
        ion_change = ion_change - (charge / cell_length) * along_z[:, None, None] * along_x[None, :, None] * along_y[None, None, :]

    effective = ion_potential + exchange_potential
    change = exchange_kernel * response + hartree + ion_change
    kinetic = 0.5 * factor * radius.astype(jnp.float32)

    def apply_band(couple):
        first = real_field(couple[0])
        second = real_field(couple[1])
        product = effective * second + change * first
        spectrum = jnp.fft.fftn(product).reshape(N, N * N)[:, stick_columns] / (weight * N ** 3)
        tangent_coeff = couple[1] * sphere
        result_real = (jnp.real(spectrum) + kinetic * tangent_coeff[0]) * sphere
        result_imag = (jnp.imag(spectrum) + kinetic * tangent_coeff[1]) * sphere
        return jnp.stack([result_real, result_imag])

    return lax.map(apply_band, (orbitals, orbital_tangent))
```

```python
import functools
import math

import jax
import jax.numpy as jnp
import ml_dtypes
import numpy as np
from jax import lax
from jax.experimental import pallas as pl
from jax.experimental.pallas import tpu as pltpu
from jax.sharding import Mesh, PartitionSpec as P

N = 128
BANDS = 32
STICKS = 4096
DISP = 8
CUT = N // 4
LINE = 72
SLABS = 68
CELLS = SLABS * LINE
DUMP = 65 * LINE
CELL = 40.0
SLATER = (3.0 / math.pi) ** (1.0 / 3.0)
FACTOR = (2.0 * math.pi / CELL) ** 2
WEIGHT = 4.0 / N**1.5

BAND_AXES = ("xl", "yh", "yl", "core")
GA_AXES = ("xh", "z")
PLANE_AXES = ("xl", "yl", "core", "xh", "z")
SUBS = 8
GROUPS = 16

f32 = jnp.float32
bf16 = jnp.bfloat16


def split_table(table):
    table = np.asarray(table, np.float64)
    high = table.astype(np.float32).astype(ml_dtypes.bfloat16)
    low = (table - high.astype(np.float64)).astype(np.float32).astype(ml_dtypes.bfloat16)
    return np.stack([high, low])


def signed(values):
    return np.where(values >= N // 2, values - N, values)


def angles(rows, columns):
    return 2.0 * np.pi * (np.outer(rows, columns) % N) / N


def plane_of_holder():
    holder = np.arange(N)
    return (holder % GROUPS) * SUBS + holder // GROUPS


def z_inverse_table():
    kept = np.concatenate([np.arange(0, 40), np.arange(96, 128)])
    angle = angles(plane_of_holder(), kept)
    inside = np.abs(signed(kept)) <= CUT
    cosine, sine = np.cos(angle) * inside, np.sin(angle) * inside
    return split_table(np.block([[cosine, -sine], [sine, cosine]]))


def z_forward_table():
    kept = np.concatenate([np.arange(0, 40), np.arange(96, 128)])
    angle = angles(kept, plane_of_holder())
    scale = 1.0 / (WEIGHT * N**3)
    cosine, sine = np.cos(angle) * scale, np.sin(angle) * scale
    return split_table(np.block([[cosine, sine], [-sine, cosine]]))


def box_frequencies(count):
    slot = np.arange(count)
    return slot - CUT, (slot <= 2 * CUT).astype(np.float64)


def y_inverse_table():
    frequency, kept = box_frequencies(LINE)
    angle = angles(frequency, np.arange(N))
    return split_table(np.concatenate([np.cos(angle), np.sin(angle)], 1) * kept[:, None])


def x_inverse_table():
    across = (4 * np.arange(24)[None, :] + np.arange(4)[:, None]).reshape(-1)
    kept = (across <= 2 * CUT).astype(np.float64)
    angle = angles(np.arange(N), across - CUT)
    cosine, sine = WEIGHT * np.cos(angle) * kept, WEIGHT * np.sin(angle) * kept
    return split_table(np.block([[cosine, -sine], [sine, cosine]]))


def x_forward_table():
    frequency, kept = box_frequencies(LINE)
    angle = angles(frequency, np.arange(N))
    cosine, sine = np.cos(angle) * kept[:, None], np.sin(angle) * kept[:, None]
    return split_table(np.block([[cosine, sine], [-sine, cosine]]))


def y_forward_table():
    frequency, kept = box_frequencies(N)
    angle = angles(np.arange(N), frequency)
    return split_table(np.concatenate([np.cos(angle), np.sin(angle)], 1) * np.concatenate([kept, kept])[None, :])


def spread_table():
    table = np.zeros((N, 8, N))
    for band in range(8):
        for part in range(2):
            for eighth in range(8):
                for group in range(4):
                    for half in range(2):
                        table[band * 16 + part * 8 + eighth, eighth, band * 16 + group * 4 + part * 2 + half] = 1.0
    table = table.reshape(N, 8 * N)
    return np.concatenate([table, table]).astype(ml_dtypes.bfloat16)


def real_table():
    row = np.arange(N)
    frequency = np.where(row <= N // 2, row, row - N // 2)
    angle = angles(frequency, np.arange(N))
    values = np.where((row <= N // 2)[:, None], np.cos(angle), np.sin(angle))
    scale = np.where((row == 0) | (row == N // 2), math.sqrt(1.0 / N), math.sqrt(2.0 / N))
    return values * scale[:, None]


def profile_table():
    frequency = np.arange(N) - N // 2
    angle = angles(frequency, np.arange(N))
    return split_table(np.concatenate([np.cos(angle), np.sin(angle)]))


def halves(values):
    high = values.astype(bf16)
    return high, (values - high.astype(f32)).astype(bf16)


def dot(a, b, dims=((1,), (0,))):
    return lax.dot_general(a, b, (dims, ((), ())), preferred_element_type=f32)


def dot3(left, right, dims=((1,), (0,))):
    return dot(left[0], right[0], dims) + (dot(left[0], right[1], dims) + dot(left[1], right[0], dims))


def pair(ref):
    return ref[0], ref[1]


def stick_frequencies(columns):
    across = columns >> 7
    inplane = columns & (N - 1)
    across = jnp.where(across >= N // 2, across - N, across)
    inplane = jnp.where(inplane >= N // 2, inplane - N, inplane)
    return across, inplane


def kept_rows(shape):
    row = lax.broadcasted_iota(jnp.int32, shape, 0)
    return jnp.where(row >= 40, row + 56 - N, row)


def sphere_radius(columns):
    across, inplane = stick_frequencies(columns)
    frequency = kept_rows((LINE, columns.shape[1]))
    return frequency * frequency + (across * across + inplane * inplane)


def lines_kernel(orbital_ref, tangent_ref, columns_ref, table_ref, out_ref):
    inside = sphere_radius(columns_ref[...]) <= CUT * CUT
    for which, ref in enumerate((orbital_ref, tangent_ref)):
        parts = []
        for part in range(2):
            kept = jnp.concatenate([ref[0, part, 0:40, :], ref[0, part, 96:128, :]], 0)
            parts.append(jnp.where(inside, kept, 0.0))
        lines = dot3(pair(table_ref), halves(jnp.concatenate(parts, 0)))
        for part in range(2):
            for half in range(2):
                row = half * 4 + which * 2 + part
                out_ref[pl.ds(row, N, stride=8), :] = lines[part * N : (part + 1) * N, half * N : (half + 1) * N]


def fields_kernel(
    dest_ref, lines_ref, ytable_ref, xtable_ref, real_ref, realt_ref, fields_ref, sums_ref, spectrum_ref, turned, grid, ycos, ysin
):
    for block in range(8):
        tiles = [lines_ref[sub * GROUPS + 2 * block + odd] for odd in range(2) for sub in range(SUBS)]
        turned[block * N : (block + 1) * N, :] = jnp.concatenate(tiles, 0).T
    grid[...] = jnp.zeros_like(grid)
    lane = lax.broadcasted_iota(jnp.int32, (1, N), 1)
    group = (lane // 64) * 2 + (lane // 4) % 2
    masks = [group == slot for slot in range(4)]
    for block in range(8):

        def scatter(step, carry, block=block):
            for inner in range(8):
                stick = step * 8 + inner
                row = turned[pl.ds(block * N + stick, 1), :]
                for slot in range(4):
                    place = dest_ref[(2 * block + slot // 2) * 256 + (slot % 2) * N + stick]
                    grid[pl.ds(place, 1), :] = jnp.where(masks[slot], row, 0.0)
            return carry

        lax.fori_loop(0, N // 8, scatter, 0)
    lane = lax.broadcasted_iota(jnp.int32, (LINE, N), 1)
    group = (lane // 64) * 2 + (lane // 4) % 2
    first_half = (lane // 4) % 2 == 0
    blank = jnp.zeros((N, N), f32)
    for step in range(17, 24):
        ycos[step * N : (step + 1) * N, :] = blank
        ysin[step * N : (step + 1) * N, :] = blank

    ytable = pair(ytable_ref)
    for step in range(17):
        packed = None
        for slot in range(4):
            slab = grid[(4 * step + slot) * LINE : (4 * step + slot + 1) * LINE, :]
            slab = slab + pltpu.roll(slab, 64, 1)
            slab = slab + jnp.where(first_half, pltpu.roll(slab, N - 4, 1), pltpu.roll(slab, 4, 1))
            packed = slab if packed is None else jnp.where(group == slot, slab, packed)
        lines = dot3(halves(packed.T), ytable)
        ycos[step * N : (step + 1) * N, :] = lines[:, 0:N]
        ysin[step * N : (step + 1) * N, :] = lines[:, N : 2 * N]
    density = jnp.zeros((N, N), f32)
    response = jnp.zeros((N, N), f32)
    xtable = pair(xtable_ref)
    for band in range(SUBS):
        sides = []
        for which in range(2):
            real, imag = [], []
            for slot in range(4):
                base = (slot // 2) * 64 + band * 8 + (slot % 2) * 4 + which * 2
                rows = [pl.ds(base + part, 24, stride=N) for part in range(2)]
                real.append(ycos[rows[0], :] - ysin[rows[1], :])
                imag.append(ysin[rows[0], :] + ycos[rows[1], :])
            sides.append(jnp.concatenate(real + imag, 0))
        field = dot3(xtable, halves(jnp.concatenate(sides, 1)))
        fields_ref[band] = field
        first, second = field[:, 0:N], field[:, N : 2 * N]
        density = density + first[0:N] * first[0:N] + first[N : 2 * N] * first[N : 2 * N]
        response = response + first[0:N] * second[0:N] + first[N : 2 * N] * second[N : 2 * N]
    response = response * (2.0 / BANDS)
    sums_ref[0] = density * (1.0 / BANDS)
    sums_ref[1] = response
    spectrum_ref[...] = dot3(halves(dot3(pair(real_ref), halves(response))), pair(realt_ref))


def hartree_kernel(place_ref, columns_ref, real_ref, back_ref, out_ref):
    four = [columns_ref[pl.ds(slot, N, stride=4), :] for slot in range(4)]
    lines = dot3(pair(real_ref), halves(jnp.concatenate(four, 1)))
    shape = (N, 4 * N)
    row = lax.broadcasted_iota(jnp.int32, shape, 0)
    lane = lax.broadcasted_iota(jnp.int32, shape, 1)
    across = place_ref[0] * 4 + lane // N
    inplane = lane % N

    def frequency(index):
        return jnp.where(index <= N // 2, index, index - N // 2)

    across, inplane, row = frequency(across), frequency(inplane), frequency(row)
    squares = (row * row + across * across + inplane * inplane).astype(f32)
    kernel = jnp.where(squares == 0.0, 0.0, (4.0 * math.pi / FACTOR) / jnp.where(squares == 0.0, 1.0, squares))
    back = dot3(halves(back_ref[...]), halves(lines * kernel))
    for slot in range(4):
        part = back[:, slot * N : (slot + 1) * N]
        for copy in range(4):
            for x_low in range(2):
                base = ((x_low * 4 + copy) * 4) * 4 + slot
                out_ref[pl.ds(base, 4, stride=4), :] = part[x_low * 4 : (x_low + 1) * 4]


def ions_kernel(place_ref, atom_ref, direction_ref, positions_ref, charge_ref, widths_ref, table_ref, out_ref, centres, spreads, marks, charges):
    for slot in range(DISP):
        atom = atom_ref[slot]
        charges[slot : slot + 1, :] = jnp.full((1, N), charge_ref[atom] * (-1.0 / CELL), f32)
        for axis in range(3):
            row = axis * DISP + slot
            centres[row : row + 1, :] = jnp.full((1, N), positions_ref[atom * 3 + axis], f32)
            spreads[row : row + 1, :] = jnp.full((1, N), widths_ref[atom], f32)
            marks[row : row + 1, :] = jnp.full((1, N), jnp.where(direction_ref[slot] == axis, 1.0, 0.0), f32)
    frequency = lax.broadcasted_iota(jnp.int32, (3 * DISP, N), 1) - N // 2
    wavenum = frequency.astype(f32) * (2.0 * math.pi / CELL)
    damping = jnp.exp(-0.5 * (wavenum * spreads[...]) ** 2)
    phase = wavenum * centres[...]
    cosine, sine = damping * jnp.cos(phase), damping * jnp.sin(phase)
    chosen = marks[...] > 0.5
    with_cos = jnp.where(chosen, -wavenum * sine, cosine)
    with_sin = jnp.where(chosen, wavenum * cosine, sine)
    profiles = dot3(halves(jnp.concatenate([with_cos, with_sin], 1)), pair(table_ref))
    along_x, along_y, along_z = profiles[0:8], profiles[8:16], profiles[16:24]
    lane = lax.broadcasted_iota(jnp.int32, (DISP, N), 1)
    here = jnp.sum(jnp.where(lane == place_ref[1], along_z, 0.0), 1, keepdims=True)
    scaled = along_y * here * charges[...]
    padding = jnp.zeros((N - DISP, N), f32)
    left = jnp.concatenate([along_x, padding], 0).T
    right = jnp.concatenate([scaled, padding], 0)
    out_ref[...] = dot3(halves(left), halves(right))


def products_kernel(
    place_ref,
    dest_ref,
    fields_ref,
    sums_ref,
    hartree_ref,
    ions_ref,
    potential_ref,
    core_ref,
    real_ref,
    realt_ref,
    xtable_ref,
    ytable_ref,
    spread_ref,
    out_ref,
    lines,
    grid,
    gathered,
):
    density = (sums_ref[0, 0] + sums_ref[1, 0]) + (sums_ref[2, 0] + sums_ref[3, 0])
    response = (sums_ref[0, 1] + sums_ref[1, 1]) + (sums_ref[2, 1] + sums_ref[3, 1])
    hartree = dot3(halves(dot3(pair(realt_ref), halves(hartree_ref[...]))), pair(real_ref))
    total = density + core_ref[0]
    root = jnp.exp(jnp.log(total) * (1.0 / 3.0))
    exchange = -SLATER * root
    effective = potential_ref[0] + exchange
    change = exchange / (3.0 * total) * response + hartree + ions_ref[...]
    xtable = pair(xtable_ref)
    ytable = pair(ytable_ref)
    effective2 = jnp.concatenate([effective, effective], 0)
    change2 = jnp.concatenate([change, change], 0)
    blocks = [[], []]
    for couple in range(SUBS // 2):
        sides = []
        for band in (2 * couple, 2 * couple + 1):
            sides.append(effective2 * fields_ref[band, :, N : 2 * N] + change2 * fields_ref[band, :, 0:N])
        across = dot3(xtable, halves(jnp.concatenate(sides, 1)))
        rows = jnp.concatenate([across[:, 0:N], across[:, N : 2 * N]], 0)
        done = dot3(halves(rows), ytable)
        for side in range(2):
            real = done[side * 144 : side * 144 + 72]
            imag = done[side * 144 + 72 : side * 144 + 144]
            base = (2 * couple + side) * 144
            lines[base : base + 72, :] = real[:, 0:N] + imag[:, N : 2 * N]
            lines[base + 72 : base + 144, :] = imag[:, 0:N] - real[:, N : 2 * N]
    spread = spread_ref[...]
    for eight in range(9):
        tiles = [lines[half * 72 + eight * 8 : half * 72 + eight * 8 + 8, :] for half in range(16)]
        turned = jnp.concatenate(tiles, 0).T[0:LINE]
        high, low = halves(turned)
        cells = dot(jnp.concatenate([high, low], 1), spread)
        for eighth in range(8):
            base = (eight * 8 + eighth) * LINE
            grid[base : base + LINE, :] = cells[:, eighth * N : (eighth + 1) * N]
    lane = lax.broadcasted_iota(jnp.int32, (1, N), 1)
    slot_of_lane = ((lane // 4) % 4) * 2 + lane % 2
    masks = [slot_of_lane == slot for slot in range(1, 8)]
    for block in range(4):

        def gather(step, carry, block=block):
            for inner in range(8):
                stick = step * 8 + inner
                row = None
                for slot in range(8):
                    place = dest_ref[(4 * block + slot // 2) * 256 + (slot % 2) * N + stick]
                    cell = grid[pl.ds(place, 1), :]
                    row = cell if slot == 0 else jnp.where(masks[slot - 1], cell, row)
                gathered[pl.ds(stick, 1), :] = row
            return carry

        lax.fori_loop(0, N // 8, gather, 0)
        turned = gathered[...].T
        for band in range(SUBS):
            base = band * 64 + block * 16
            out_ref[base : base + 16, :] = turned[band * 16 : band * 16 + 16]


def result_kernel(arrived_ref, tangent_ref, columns_ref, table_ref, out_ref):
    sides = []
    for half in range(2):
        parts = [arrived_ref[pl.ds(part * 2 + half, N, stride=4), :] for part in range(2)]
        sides.append(jnp.concatenate(parts, 0))
    lines = dot3(pair(table_ref), halves(jnp.concatenate(sides, 1)))
    radius = sphere_radius(columns_ref[...])
    inside = radius <= CUT * CUT
    kinetic = (0.5 * FACTOR) * radius.astype(f32)
    for part in range(2):
        kept = jnp.concatenate([tangent_ref[0, part, 0:40, :], tangent_ref[0, part, 96:128, :]], 0)
        rows = jnp.where(inside, lines[part * LINE : (part + 1) * LINE] + kinetic * kept, 0.0)
        out_ref[0, part, 0:40, :] = rows[0:40]
        out_ref[0, part, 40:96, :] = jnp.zeros((56, 256), f32)
        out_ref[0, part, 96:128, :] = rows[40:72]


def vmem(count):
    return [pl.BlockSpec(memory_space=pltpu.VMEM)] * count


def smem(count):
    return [pl.BlockSpec(memory_space=pltpu.SMEM)] * count


def shape(*dims):
    return jax.ShapeDtypeStruct(dims, f32)


def params(mebibytes):
    return pltpu.CompilerParams(vmem_limit_bytes=mebibytes << 20)


def body(
    orbitals,
    orbital_tangent,
    stick_columns,
    ion_potential,
    core_density,
    positions,
    z_charge,
    widths,
    atom_index,
    direction,
):
    group = lax.axis_index(GA_AXES)
    member = lax.axis_index(BAND_AXES)
    sub = lax.axis_index(("xl", "yl", "core"))
    plane = group * SUBS + sub
    place = jnp.stack([member, plane]).astype(jnp.int32)
    columns = lax.dynamic_slice_in_dim(stick_columns, group * 256, 256).reshape(1, 256)
    across, inplane = stick_frequencies(stick_columns)
    cell = (across + CUT) * LINE + (inplane + CUT)
    dest = jnp.where(across * across + inplane * inplane <= CUT * CUT, cell, DUMP)
    real = split_table(real_table())
    realt = split_table(real_table().T)

    lines = pl.pallas_call(
        lines_kernel, out_shape=shape(N * 8, N), in_specs=vmem(4), out_specs=vmem(1)[0], name="lines"
    )(orbitals, orbital_tangent, columns, z_inverse_table())
    lines = lax.all_to_all(lines.reshape(N, 8, N), PLANE_AXES, 0, 0, tiled=True)
    ions = pl.pallas_call(
        ions_kernel,
        out_shape=shape(N, N),
        in_specs=smem(6) + vmem(1),
        out_specs=vmem(1)[0],
        scratch_shapes=[pltpu.VMEM((24, N), f32)] * 3 + [pltpu.VMEM((8, N), f32)],
        name="ions",
    )(place, atom_index, direction, positions.reshape(-1), z_charge, widths, profile_table())
    fields, sums, spectrum = pl.pallas_call(
        fields_kernel,
        out_shape=(shape(SUBS, 2 * N, 2 * N), shape(2, N, N), shape(N, N)),
        in_specs=smem(1) + vmem(5),
        out_specs=tuple(vmem(3)),
        scratch_shapes=[
            pltpu.VMEM((8 * N, N), f32),
            pltpu.VMEM((CELLS, N), f32),
            pltpu.VMEM((24 * N, N), f32),
            pltpu.VMEM((24 * N, N), f32),
        ],
        compiler_params=params(32),
        name="fields",
    )(dest, lines, y_inverse_table(), x_inverse_table(), real, realt)
    sums = lax.all_gather(sums, "yh")
    arrived = lax.all_to_all(spectrum.reshape(32, 4, N), BAND_AXES, 0, 0, tiled=True)
    arrived = arrived.reshape(2, 4, 4, 4, N).sum(1).reshape(1, 8 * 4, N)
    arrived = jnp.broadcast_to(arrived, (GROUPS, 32, N))
    columns_here = lax.all_to_all(arrived, GA_AXES, 0, 0, tiled=True).reshape(4 * N, N)
    back = lax.dynamic_slice_in_dim(jnp.asarray(real_table().T, f32), group * SUBS, SUBS)
    solved = pl.pallas_call(
        hartree_kernel,
        out_shape=shape(N, N),
        in_specs=smem(1) + vmem(3),
        out_specs=vmem(1)[0],
        name="hartree",
    )(place, columns_here, real, back)
    solved = lax.all_to_all(solved.reshape(32, 4, N), BAND_AXES, 0, 0, tiled=True).reshape(N, N)
    potential = lax.dynamic_slice_in_dim(ion_potential, sub, 1)
    core = lax.dynamic_slice_in_dim(core_density, sub, 1)
    outgoing = pl.pallas_call(
        products_kernel,
        out_shape=shape(4 * N, N),
        in_specs=smem(2) + vmem(11),
        out_specs=vmem(1)[0],
        scratch_shapes=[
            pltpu.VMEM((16 * LINE, N), f32),
            pltpu.VMEM((LINE * LINE, N), f32),
            pltpu.VMEM((N, N), f32),
        ],
        compiler_params=params(32),
        name="products",
    )(
        place,
        dest,
        fields,
        sums,
        solved,
        ions,
        potential,
        core,
        real,
        realt,
        x_forward_table(),
        y_forward_table(),
        spread_table(),
    )
    arrived = lax.all_to_all(outgoing.reshape(N, 4, N), PLANE_AXES, 0, 0, tiled=True).reshape(4 * N, N)
    return pl.pallas_call(
        result_kernel, out_shape=shape(1, 2, N, 256), in_specs=vmem(4), out_specs=vmem(1)[0], name="result"
    )(arrived, orbital_tangent, columns, z_forward_table())


def solution(mesh):
    fine = Mesh(mesh.devices.reshape(2, 4, 2, 2, 2, 8), BAND_AXES + GA_AXES)
    lines = P(BAND_AXES, None, None, GA_AXES)
    planes = P(GA_AXES, None, None)
    return jax.shard_map(
        body,
        mesh=fine,
        in_specs=(lines, lines, P(), planes, planes, P(), P(), P(), P(), P()),
        out_specs=lines,
        check_vma=False,
    )
```

```python
import functools
import math

import jax
import jax.numpy as jnp
import ml_dtypes
import numpy as np
from jax import lax
from jax.experimental import pallas as pl
from jax.experimental.pallas import tpu as pltpu
from jax.sharding import Mesh, PartitionSpec as P

N = 128
BANDS = 32
STICKS = 4096
DISP = 8
CUT = N // 4
LINE = 72
SLABS = 68
CELLS = SLABS * LINE
DUMP = 65 * LINE
CELL = 40.0
SLATER = (3.0 / math.pi) ** (1.0 / 3.0)
FACTOR = (2.0 * math.pi / CELL) ** 2
WEIGHT = 4.0 / N**1.5

BAND_AXES = ("xl", "yh", "yl", "core")
GA_AXES = ("xh", "z")
PLANE_AXES = ("xl", "yl", "core", "xh", "z")
SUBS = 8
PITCH = 136
GROUPS = 16

f32 = jnp.float32
bf16 = jnp.bfloat16


def split_table(table):
    table = np.asarray(table, np.float64)
    high = table.astype(np.float32).astype(ml_dtypes.bfloat16)
    low = (table - high.astype(np.float64)).astype(np.float32).astype(ml_dtypes.bfloat16)
    return np.stack([high, low])


def signed(values):
    return np.where(values >= N // 2, values - N, values)


def angles(rows, columns):
    return 2.0 * np.pi * (np.outer(rows, columns) % N) / N


def plane_of_holder():
    holder = np.arange(N)
    return (holder % GROUPS) * SUBS + holder // GROUPS


def z_inverse_table():
    kept = np.concatenate([np.arange(0, 40), np.arange(96, 128)])
    angle = angles(plane_of_holder(), kept)
    inside = np.abs(signed(kept)) <= CUT
    cosine, sine = np.cos(angle) * inside, np.sin(angle) * inside
    return split_table(np.block([[cosine, -sine], [sine, cosine]]))


def z_forward_table():
    kept = np.concatenate([np.arange(0, 40), np.arange(96, 128)])
    angle = angles(kept, plane_of_holder())
    scale = 1.0 / (WEIGHT * N**3)
    cosine, sine = np.cos(angle) * scale, np.sin(angle) * scale
    return split_table(np.block([[cosine, sine], [-sine, cosine]]))


def box_frequencies(count):
    slot = np.arange(count)
    return slot - CUT, (slot <= 2 * CUT).astype(np.float64)


def y_inverse_table():
    frequency, kept = box_frequencies(LINE)
    angle = angles(frequency, np.arange(N))
    return (np.concatenate([np.cos(angle), np.sin(angle)], 1) * kept[:, None])


def x_inverse_table():
    across = (4 * np.arange(24)[None, :] + np.arange(4)[:, None]).reshape(-1)
    kept = (across <= 2 * CUT).astype(np.float64)
    angle = angles(np.arange(N), across - CUT)
    cosine, sine = WEIGHT * np.cos(angle) * kept, WEIGHT * np.sin(angle) * kept
    return (np.block([[cosine, -sine], [sine, cosine]]))


def x_forward_table():
    frequency, kept = box_frequencies(LINE)
    angle = angles(frequency, np.arange(N))
    cosine, sine = np.cos(angle) * kept[:, None], np.sin(angle) * kept[:, None]
    return (np.block([[cosine, sine], [-sine, cosine]]))


def y_forward_table():
    frequency, kept = box_frequencies(N)
    angle = angles(np.arange(N), frequency)
    return (np.concatenate([np.cos(angle), np.sin(angle)], 1) * np.concatenate([kept, kept])[None, :])


def spread_table():
    table = np.zeros((N, 8, N))
    for band in range(8):
        for part in range(2):
            for eighth in range(8):
                for group in range(4):
                    for half in range(2):
                        table[band * 16 + part * 8 + eighth, eighth, band * 16 + group * 4 + part * 2 + half] = 1.0
    table = table.reshape(N, 4, 2 * N).transpose(1, 0, 2)
    return np.concatenate([table, table], 1).reshape(8 * N, 2 * N)


def real_table():
    row = np.arange(N)
    frequency = np.where(row <= N // 2, row, row - N // 2)
    angle = angles(frequency, np.arange(N))
    values = np.where((row <= N // 2)[:, None], np.cos(angle), np.sin(angle))
    scale = np.where((row == 0) | (row == N // 2), math.sqrt(1.0 / N), math.sqrt(2.0 / N))
    return values * scale[:, None]


def profile_table():
    frequency = np.arange(N) - N // 2
    angle = angles(frequency, np.arange(N))
    return split_table(np.concatenate([np.cos(angle), np.sin(angle)]))


def packed_tables(named, exact={}):
    blocks, places, row = [], {}, 0
    for name, table in named.items():
        parts = split_table(table)
        rows, columns = parts.shape[1:]
        tall = -(-rows // 16) * 16
        block = np.zeros((2, tall, 256), ml_dtypes.bfloat16)
        block[:, :rows, :columns] = parts
        blocks.append(block.reshape(2 * tall, 256))
        places[name] = (row, row + tall, rows, columns)
        row += 2 * tall
    for name, table in exact.items():
        blocks.append(table.astype(ml_dtypes.bfloat16))
        places[name] = row
        row += table.shape[0]
    return np.concatenate(blocks), places


def holder_planes():
    holder = np.arange(N)
    return ((holder % 2) * 8 + holder // 16) * SUBS + (holder // 2) % 8


def early_tables():
    return packed_tables(
        {
            "y_inverse": y_inverse_table(),
            "x_inverse": x_inverse_table(),
            "real": real_table(),
            "real_turned": real_table().T,
        }
    )


def late_tables():
    return packed_tables(
        {
            "real_planes": real_table()[:, holder_planes()],
            "planes_real": real_table().T[holder_planes()],
            "real": real_table(),
            "real_turned": real_table().T,
            "x_forward": x_forward_table(),
            "y_forward": y_forward_table(),
        },
        {"spread": spread_table()},

    )


EARLY, EARLY_PLACES = early_tables()
LATE, LATE_PLACES = late_tables()


def table_of(ref, places, name):
    high, low, rows, columns = places[name]
    return ref[high : high + rows, 0:columns], ref[low : low + rows, 0:columns]


def early_table(ref, name):
    return table_of(ref, EARLY_PLACES, name)


def late_table(ref, name):
    return table_of(ref, LATE_PLACES, name)


def halves(values):
    high = values.astype(bf16)
    return high, (values - high.astype(f32)).astype(bf16)


def dot(a, b, dims=((1,), (0,))):
    return lax.dot_general(a, b, (dims, ((), ())), preferred_element_type=f32)


def dot3(left, right, dims=((1,), (0,))):
    return dot(left[0], right[0], dims) + (dot(left[0], right[1], dims) + dot(left[1], right[0], dims))


def pair(ref):
    return ref[0], ref[1]


def stick_frequencies(columns):
    across = columns >> 7
    inplane = columns & (N - 1)
    across = jnp.where(across >= N // 2, across - N, across)
    inplane = jnp.where(inplane >= N // 2, inplane - N, inplane)
    return across, inplane


def kept_rows(shape):
    row = lax.broadcasted_iota(jnp.int32, shape, 0)
    return jnp.where(row >= 40, row + 56 - N, row)


def sphere_radius(columns):
    across, inplane = stick_frequencies(columns)
    frequency = kept_rows((LINE, columns.shape[1]))
    return frequency * frequency + (across * across + inplane * inplane)


def own_columns(columns_ref):
    group = lax.axis_index(GA_AXES)
    return jnp.concatenate([columns_ref[pl.ds(2 * group + half, 1), :] for half in range(2)], 1)


def lines_kernel(orbital_ref, tangent_ref, columns_ref, table_ref, out_ref):
    inside = sphere_radius(own_columns(columns_ref)) <= CUT * CUT
    for which, ref in enumerate((orbital_ref, tangent_ref)):
        parts = []
        for part in range(2):
            kept = jnp.concatenate([ref[0, part, 0:40, :], ref[0, part, 96:128, :]], 0)
            parts.append(jnp.where(inside, kept, 0.0))
        lines = dot3(pair(table_ref), halves(jnp.concatenate(parts, 0)))
        for part in range(2):
            for half in range(2):
                row = half * 4 + which * 2 + part
                out_ref[pl.ds(row, N, stride=8), :] = lines[part * N : (part + 1) * N, half * N : (half + 1) * N]


def fields_kernel(
    dest_ref,
    lines_ref,
    ions_ref,
    potential_ref,
    core_ref,
    early_ref,
    late_ref,
    fields_ref,
    sums_ref,
    planes_ref,
    late_out,
    turned,
    grid,
    ycos,
    ysin,
    tables,
    arrivals,
):
    own = lax.axis_index(("xl", "yl", "core"))
    copies = [
        pltpu.make_async_copy(early_ref, tables, arrivals.at[0]),
        pltpu.make_async_copy(late_ref, late_out, arrivals.at[1]),
        pltpu.make_async_copy(potential_ref.at[own], planes_ref.at[0], arrivals.at[2]),
        pltpu.make_async_copy(core_ref.at[own], planes_ref.at[1], arrivals.at[3]),
    ]
    for copy in copies:
        copy.start()
    planes_ref[2] = ions_ref[...]
    lower = lax.broadcasted_iota(jnp.int32, (8, N), 0) < 4
    for quad in range(4):
        for half in range(2):
            tiles = []
            for group in range(4 * quad, 4 * quad + 4):
                for sub in range(0, SUBS, 2):
                    first, second = lines_ref[sub * GROUPS + group], lines_ref[(sub + 1) * GROUPS + group]
                    if half == 0:
                        tiles.append(jnp.where(lower, first, pltpu.roll(second, 4, 0)))
                    else:
                        tiles.append(jnp.where(lower, pltpu.roll(first, 4, 0), second))
            base = (quad * 2 + half) * N
            turned[base : base + N, :] = jnp.concatenate(tiles, 0).T
    grid[...] = jnp.zeros_like(grid)
    lane = lax.broadcasted_iota(jnp.int32, (1, N), 1)
    masks = [lane // 32 == slot for slot in range(4)]
    for quad in range(4):

        def scatter(step, carry, quad=quad):
            for inner in range(8):
                stick = step * 8 + inner
                rows = [turned[pl.ds((quad * 2 + half) * N + stick, 1), :] for half in range(2)]
                for slot in range(4):
                    places = dest_ref[(4 * quad + slot) * N + stick]
                    grid[pl.ds(places & 0xFFFF, 1), :] = jnp.where(masks[slot], rows[0], 0.0)
                    grid[pl.ds(places >> 16, 1), :] = jnp.where(masks[slot], rows[1], 0.0)
            return carry

        lax.fori_loop(0, N // 8, scatter, 0)
    lane = lax.broadcasted_iota(jnp.int32, (LINE, N), 1)
    masks = [lane // 32 == slot for slot in range(4)]
    blank = jnp.zeros((N, N), f32)
    for step in range(17, 24):
        ycos[step * PITCH : step * PITCH + N, :] = blank
        ysin[step * PITCH : step * PITCH + N, :] = blank

    copies[0].wait()
    ytable = early_table(tables, "y_inverse")
    for step in range(17):
        packed = None
        for slot in range(4):
            slab = grid[(4 * step + slot) * LINE : (4 * step + slot + 1) * LINE, :]
            slab = slab + pltpu.roll(slab, 64, 1)
            slab = slab + pltpu.roll(slab, 32, 1)
            packed = slab if packed is None else jnp.where(masks[slot], slab, packed)
        lines = dot3(halves(packed.T), ytable)
        ycos[step * PITCH : step * PITCH + N, :] = lines[:, 0:N]
        ysin[step * PITCH : step * PITCH + N, :] = lines[:, N : 2 * N]
    density = jnp.zeros((N, N), f32)
    response = jnp.zeros((N, N), f32)
    xtable = early_table(tables, "x_inverse")
    for band in range(SUBS):
        sides = []
        for which in range(2):
            real, imag = [], []
            for slot in range(4):
                base = slot * 32 + band * 4 + which * 2
                rows = [pl.ds(base + part, 24, stride=PITCH) for part in range(2)]
                real.append(ycos[rows[0], :] - ysin[rows[1], :])
                imag.append(ysin[rows[0], :] + ycos[rows[1], :])
            sides.append(jnp.concatenate(real + imag, 0))
        field = dot3(xtable, halves(jnp.concatenate(sides, 1)))
        fields_ref[band] = field
        first, second = field[:, 0:N], field[:, N : 2 * N]
        density = density + first[0:N] * first[0:N] + first[N : 2 * N] * first[N : 2 * N]
        response = response + first[0:N] * second[0:N] + first[N : 2 * N] * second[N : 2 * N]
    density = density * (1.0 / BANDS)
    response = response * (2.0 / BANDS)
    spectrum = dot3(
        halves(dot3(early_table(tables, "real"), halves(response))), early_table(tables, "real_turned")
    )
    for half in range(2):
        sums_ref[pl.ds(half, 64, stride=4), :] = density[half * 64 : half * 64 + 64]
        sums_ref[pl.ds(2 + half, 64, stride=4), :] = spectrum[half * 64 : half * 64 + 64]
    for copy in copies[1:]:
        copy.wait()


def mix_kernel(arrived_ref, sums_ref, spread_ref):
    for x_low in range(2):
        base = x_low * 128
        rows = [arrived_ref[base + copy * 32 : base + copy * 32 + 32, :] for copy in range(4)]
        sums_ref[x_low * 32 : x_low * 32 + 32, :] = (rows[0] + rows[1]) + (rows[2] + rows[3])
    spectrum = [sums_ref[pl.ds(2 + half, 16, stride=4), :] for half in range(2)]
    for copy in range(8):
        for half in range(2):
            base = copy * 32 + half * 16
            spread_ref[base : base + 16, :] = spectrum[half]


def hartree_kernel(sums_ref, columns_ref, tables_ref, out_ref):
    sides = []
    for half in range(2):
        sides.append(jnp.concatenate([columns_ref[z * 32 + half * 16 : z * 32 + half * 16 + 16, :] for z in range(8)], 0))
    lines = dot3(late_table(tables_ref, "real_planes"), halves(jnp.concatenate(sides, 1)))
    shape = (N, 2 * N)
    row = lax.broadcasted_iota(jnp.int32, shape, 0)
    lane = lax.broadcasted_iota(jnp.int32, shape, 1)
    across = lax.axis_index(BAND_AXES) * 2 + lax.axis_index("xh") + jnp.where(lane >= N, 64, 0)
    inplane = lane & (N - 1)

    def frequency(index):
        return jnp.where(index <= N // 2, index, index - N // 2)

    across, inplane, row = frequency(across), frequency(inplane), frequency(row)
    squares = (row * row + across * across + inplane * inplane).astype(f32)
    kernel = jnp.where(squares == 0.0, 0.0, (4.0 * math.pi / FACTOR) / jnp.where(squares == 0.0, 1.0, squares))
    back = dot3(late_table(tables_ref, "planes_real"), halves(lines * kernel))
    own = lax.axis_index("z")
    mine = back[0:16]
    for z in range(1, 8):
        mine = jnp.where(own == z, back[z * 16 : z * 16 + 16], mine)
    back = mine
    for half in range(2):
        fields = [
            back[:, half * N : (half + 1) * N],
            sums_ref[pl.ds(half, 16, stride=4), :],
            sums_ref[pl.ds(2 + half, 16, stride=4), :],
        ]
        for which, field in enumerate(fields):
            for x_low in range(2):
                for copy in range(4):
                    base = (x_low * 32 + copy * 8) * 6 + which * 2 + half
                    out_ref[pl.ds(base, 8, stride=6), :] = field[x_low * 8 : x_low * 8 + 8]


def own_plane():
    return lax.axis_index(GA_AXES) * SUBS + lax.axis_index(("xl", "yl", "core"))


def ions_kernel(atom_ref, direction_ref, positions_ref, charge_ref, widths_ref, table_ref, out_ref, centres, spreads, marks, charges):
    for slot in range(DISP):
        atom = atom_ref[slot]
        charges[slot : slot + 1, :] = jnp.full((1, N), charge_ref[atom] * (-1.0 / CELL), f32)
        for axis in range(3):
            row = axis * DISP + slot
            centres[row : row + 1, :] = jnp.full((1, N), positions_ref[axis, atom], f32)
            spreads[row : row + 1, :] = jnp.full((1, N), widths_ref[atom], f32)
            marks[row : row + 1, :] = jnp.full((1, N), jnp.where(direction_ref[slot] == axis, 1.0, 0.0), f32)
    frequency = lax.broadcasted_iota(jnp.int32, (3 * DISP, N), 1) - N // 2
    wavenum = frequency.astype(f32) * (2.0 * math.pi / CELL)
    damping = jnp.exp(-0.5 * (wavenum * spreads[...]) ** 2)
    phase = wavenum * centres[...]
    cosine, sine = damping * jnp.cos(phase), damping * jnp.sin(phase)
    chosen = marks[...] > 0.5
    with_cos = jnp.where(chosen, -wavenum * sine, cosine)
    with_sin = jnp.where(chosen, wavenum * cosine, sine)
    profiles = dot3(halves(jnp.concatenate([with_cos, with_sin], 1)), pair(table_ref))
    along_x, along_y, along_z = profiles[0:8], profiles[8:16], profiles[16:24]
    lane = lax.broadcasted_iota(jnp.int32, (DISP, N), 1)
    here = jnp.sum(jnp.where(lane == own_plane(), along_z, 0.0), 1, keepdims=True)
    scaled = along_y * here * charges[...]
    padding = jnp.zeros((N - DISP, N), f32)
    left = jnp.concatenate([along_x, padding], 0).T
    right = jnp.concatenate([scaled, padding], 0)
    out_ref[...] = dot3(halves(left), halves(right))


def products_kernel(
    dest_ref,
    fields_ref,
    solved_ref,
    planes_ref,
    tables_ref,
    out_ref,
    lines,
    grid,
    gathered,
):
    def solved(which):
        return jnp.concatenate([solved_ref[pl.ds(which * 2 + half, 64, stride=6), :] for half in range(2)], 0)

    waves = dot3(late_table(tables_ref, "real_turned"), halves(jnp.concatenate([solved(0), solved(2)], 1)))
    waves = dot3(halves(jnp.concatenate([waves[:, 0:N], waves[:, N : 2 * N]], 0)), late_table(tables_ref, "real"))
    hartree, response = waves[0:N], waves[N : 2 * N]
    total = solved(1) + planes_ref[1]
    root = jnp.exp(jnp.log(total) * (1.0 / 3.0))
    exchange = -SLATER * root
    effective = planes_ref[0] + exchange
    change = exchange / (3.0 * total) * response + hartree + planes_ref[2]
    xtable = late_table(tables_ref, "x_forward")
    ytable = late_table(tables_ref, "y_forward")
    effective2 = jnp.concatenate([effective, effective], 0)
    change2 = jnp.concatenate([change, change], 0)
    blocks = [[], []]
    for couple in range(SUBS // 2):
        sides = []
        for band in (2 * couple, 2 * couple + 1):
            sides.append(effective2 * fields_ref[band, :, N : 2 * N] + change2 * fields_ref[band, :, 0:N])
        across = dot3(xtable, halves(jnp.concatenate(sides, 1)))
        rows = jnp.concatenate([across[:, 0:N], across[:, N : 2 * N]], 0)
        done = dot3(halves(rows), ytable)
        for side in range(2):
            real = done[side * 144 : side * 144 + 72]
            imag = done[side * 144 + 72 : side * 144 + 144]
            base = (2 * couple + side) * 144
            lines[base : base + 72, :] = real[:, 0:N] + imag[:, N : 2 * N]
            lines[base + 72 : base + 144, :] = imag[:, 0:N] - real[:, N : 2 * N]
    first = LATE_PLACES["spread"]
    spread = [tables_ref[first + block * 2 * N : first + (block + 1) * 2 * N, :] for block in range(4)]
    for eight in range(9):
        tiles = [lines[half * 72 + eight * 8 : half * 72 + eight * 8 + 8, :] for half in range(16)]
        turned = jnp.concatenate(tiles, 0).T[0:LINE]
        high, low = halves(turned)
        both = jnp.concatenate([high, low], 1)
        for block in range(4):
            cells = dot(both, spread[block])
            for side in range(2):
                base = (eight * 8 + block * 2 + side) * LINE
                grid[base : base + LINE, :] = cells[:, side * N : (side + 1) * N]
    lane = lax.broadcasted_iota(jnp.int32, (1, N), 1)
    slot_of_lane = ((lane // 4) % 4) * 2 + lane % 2
    masks = [slot_of_lane == slot for slot in range(1, 8)]
    for block in range(4):

        def gather(step, carry, block=block):
            for inner in range(8):
                stick = step * 8 + inner
                row = None
                for slot in range(4):
                    places = dest_ref[(4 * block + slot) * N + stick]
                    cells = [grid[pl.ds(places & 0xFFFF, 1), :], grid[pl.ds(places >> 16, 1), :]]
                    for half in range(2):
                        row = cells[half] if row is None else jnp.where(masks[2 * slot + half - 1], cells[half], row)
                gathered[pl.ds(stick, 1), :] = row
            return carry

        lax.fori_loop(0, N // 8, gather, 0)
        turned = gathered[...].T
        for band in range(SUBS):
            base = band * 64 + block * 16
            out_ref[base : base + 16, :] = turned[band * 16 : band * 16 + 16]


def result_kernel(arrived_ref, tangent_ref, columns_ref, table_ref, out_ref):
    sides = []
    for half in range(2):
        parts = [arrived_ref[pl.ds(part * 2 + half, N, stride=4), :] for part in range(2)]
        sides.append(jnp.concatenate(parts, 0))
    lines = dot3(pair(table_ref), halves(jnp.concatenate(sides, 1)))
    radius = sphere_radius(own_columns(columns_ref))
    inside = radius <= CUT * CUT
    kinetic = (0.5 * FACTOR) * radius.astype(f32)
    for part in range(2):
        kept = jnp.concatenate([tangent_ref[0, part, 0:40, :], tangent_ref[0, part, 96:128, :]], 0)
        rows = jnp.where(inside, lines[part * LINE : (part + 1) * LINE] + kinetic * kept, 0.0)
        out_ref[0, part, 0:40, :] = rows[0:40]
        out_ref[0, part, 40:96, :] = jnp.zeros((56, 256), f32)
        out_ref[0, part, 96:128, :] = rows[40:72]


def vmem(count):
    return [pl.BlockSpec(memory_space=pltpu.VMEM)] * count


def anywhere(count):
    return [pl.BlockSpec(memory_space=pltpu.HBM)] * count


def smem(count):
    return [pl.BlockSpec(memory_space=pltpu.SMEM)] * count


def shape(*dims):
    return jax.ShapeDtypeStruct(dims, f32)


def call(kernel, out_shape, in_specs, mebibytes, scratch=()):
    several = isinstance(out_shape, tuple)
    return pl.pallas_call(
        kernel,
        out_shape=out_shape,
        in_specs=in_specs,
        out_specs=tuple(vmem(len(out_shape))) if several else vmem(1)[0],
        scratch_shapes=scratch,
        compiler_params=pltpu.CompilerParams(vmem_limit_bytes=(mebibytes << 20) or None),
        name=kernel.__name__.removesuffix("_kernel"),
    )


def exchange(values, axes):
    return lax.all_to_all(values, axes, 0, 0, tiled=True)


def body(
    orbitals,
    orbital_tangent,
    stick_columns,
    ion_potential,
    core_density,
    positions,
    z_charge,
    widths,
    atom_index,
    direction,
):
    columns = stick_columns.reshape(STICKS // N, N)
    across, inplane = stick_frequencies(stick_columns)
    cell = (across + CUT) * LINE + (inplane + CUT)
    dest = jnp.where(across * across + inplane * inplane <= CUT * CUT, cell, DUMP).reshape(GROUPS, 2, N)
    dest = (dest[:, 0] + dest[:, 1] * 65536).reshape(-1)
    lines = call(lines_kernel, shape(N * 8, N), vmem(4), 0)(orbitals, orbital_tangent, columns, z_inverse_table())
    lines = exchange(lines.reshape(N, 8, N), PLANE_AXES)
    ions = call(
        ions_kernel, shape(N, N), smem(5) + vmem(1), 4, [pltpu.VMEM((24, N), f32)] * 3 + [pltpu.VMEM((8, N), f32)]
    )(atom_index, direction, positions.T, z_charge, widths, profile_table())
    fields, sums, planes, tables = call(
        fields_kernel,
        (
            shape(SUBS, 2 * N, 2 * N),
            shape(2 * N, N),
            shape(3, N, N),
            jax.ShapeDtypeStruct(LATE.shape, bf16),
        ),
        smem(1) + vmem(2) + anywhere(4),
        24,
        [
            pltpu.VMEM((8 * N, N), f32),
            pltpu.VMEM((CELLS, N), f32),
            pltpu.VMEM((24 * PITCH, N), f32),
            pltpu.VMEM((24 * PITCH, N), f32),
            pltpu.VMEM(EARLY.shape, bf16),
            pltpu.SemaphoreType.DMA((4,)),
        ],
    )(dest, lines, ions, ion_potential, core_density, EARLY, LATE)
    sums = exchange(sums.reshape(64, 4, N), BAND_AXES + ("xh",)).reshape(2 * N, N)
    sums, spectrum = call(mix_kernel, (shape(64, N), shape(2 * N, N)), vmem(1), 4)(sums)
    spectrum = exchange(spectrum.reshape(8, 32, N), "z").reshape(2 * N, N)
    solved = call(hartree_kernel, shape(3 * N, N), vmem(3), 4)(sums, spectrum, tables)
    solved = exchange(solved.reshape(64, 3, 2, N), BAND_AXES + ("xh",)).reshape(3 * N, N)
    outgoing = call(
        products_kernel,
        shape(4 * N, N),
        smem(1) + vmem(4),
        20,
        [
            pltpu.VMEM((16 * LINE, N), f32),
            pltpu.VMEM((LINE * LINE, N), f32),
            pltpu.VMEM((N, N), f32),
        ],
    )(
        dest,
        fields,
        solved,
        planes,
        tables,
    )
    arrived = exchange(outgoing.reshape(N, 4, N), PLANE_AXES).reshape(4 * N, N)
    return call(result_kernel, shape(1, 2, N, 256), vmem(4), 8)(arrived, orbital_tangent, columns, z_forward_table())


def solution(mesh):
    fine = Mesh(mesh.devices.reshape(2, 4, 2, 2, 2, 8), BAND_AXES + GA_AXES)
    lines = P(BAND_AXES, None, None, GA_AXES)
    planes = P(GA_AXES, None, None)
    return jax.shard_map(
        body,
        mesh=fine,
        in_specs=(lines, lines, P(), planes, planes, P(), P(), P(), P(), P()),
        out_specs=lines,
        check_vma=False,
    )
```

```python
import functools
import math

import jax
import jax.numpy as jnp
import ml_dtypes
import numpy as np
from jax import lax
from jax.experimental import pallas as pl
from jax.experimental.pallas import tpu as pltpu
from jax.sharding import Mesh, PartitionSpec as P

N = 128
BANDS = 32
STICKS = 4096
DISP = 8
CUT = N // 4
LINE = 72
SLABS = 68
CELLS = SLABS * LINE
DUMP = 65 * LINE
CELL = 40.0
SLATER = (3.0 / math.pi) ** (1.0 / 3.0)
FACTOR = (2.0 * math.pi / CELL) ** 2
WEIGHT = 4.0 / N**1.5

BAND_AXES = ("xl", "yh", "yl", "core")
GA_AXES = ("xh", "z")
PLANE_AXES = ("xl", "yl", "core", "xh", "z")
SUBS = 8
PITCH = 136
GROUPS = 16

f32 = jnp.float32
bf16 = jnp.bfloat16


def split_table(table):
    table = np.asarray(table, np.float64)
    high = table.astype(np.float32).astype(ml_dtypes.bfloat16)
    low = (table - high.astype(np.float64)).astype(np.float32).astype(ml_dtypes.bfloat16)
    return np.stack([high, low])


def signed(values):
    return np.where(values >= N // 2, values - N, values)


def angles(rows, columns):
    return 2.0 * np.pi * (np.outer(rows, columns) % N) / N


def plane_of_holder():
    holder = np.arange(N)
    return (holder % GROUPS) * SUBS + holder // GROUPS


def z_inverse_table():
    kept = np.concatenate([np.arange(0, 40), np.arange(96, 128)])
    angle = angles(plane_of_holder(), kept)
    inside = np.abs(signed(kept)) <= CUT
    cosine, sine = np.cos(angle) * inside, np.sin(angle) * inside
    return split_table(np.block([[cosine, -sine], [sine, cosine]]))


def z_forward_table():
    kept = np.concatenate([np.arange(0, 40), np.arange(96, 128)])
    angle = angles(kept, plane_of_holder())
    scale = 1.0 / (WEIGHT * N**3)
    cosine, sine = np.cos(angle) * scale, np.sin(angle) * scale
    return split_table(np.block([[cosine, sine], [-sine, cosine]]))


def box_frequencies(count):
    slot = np.arange(count)
    return slot - CUT, (slot <= 2 * CUT).astype(np.float64)


def y_inverse_table():
    frequency, kept = box_frequencies(LINE)
    angle = angles(frequency, np.arange(N))
    return (np.concatenate([np.cos(angle), np.sin(angle)], 1) * kept[:, None])


def x_inverse_table():
    across = (4 * np.arange(24)[None, :] + np.arange(4)[:, None]).reshape(-1)
    kept = (across <= 2 * CUT).astype(np.float64)
    angle = angles(np.arange(N), across - CUT)
    cosine, sine = WEIGHT * np.cos(angle) * kept, WEIGHT * np.sin(angle) * kept
    return (np.block([[cosine, -sine], [sine, cosine]]))


def x_forward_table():
    frequency, kept = box_frequencies(LINE)
    angle = angles(frequency, np.arange(N))
    cosine, sine = np.cos(angle) * kept[:, None], np.sin(angle) * kept[:, None]
    return (np.block([[cosine, sine], [-sine, cosine]]))


def y_forward_table():
    frequency, kept = box_frequencies(N)
    angle = angles(np.arange(N), frequency)
    return (np.concatenate([np.cos(angle), np.sin(angle)], 1) * np.concatenate([kept, kept])[None, :])


def spread_table():
    table = np.zeros((N, 8, N))
    for band in range(8):
        for part in range(2):
            for eighth in range(8):
                for group in range(4):
                    for half in range(2):
                        table[band * 16 + part * 8 + eighth, eighth, band * 16 + group * 4 + part * 2 + half] = 1.0
    table = table.reshape(N, 4, 2 * N).transpose(1, 0, 2)
    return np.concatenate([table, table], 1).reshape(8 * N, 2 * N)


def replicate_table():
    table = np.zeros((N, 4, 4, 2, 16))
    for group in range(4):
        for part in range(2):
            for entry in range(16):
                table[group * 32 + entry * 2 + part, group, :, part, entry] = 1.0
    table = table.reshape(N, 2, 2 * N).transpose(1, 0, 2)
    return np.concatenate([table, table], 1).reshape(4 * N, 2 * N)


def real_table():
    row = np.arange(N)
    frequency = np.where(row <= N // 2, row, row - N // 2)
    angle = angles(frequency, np.arange(N))
    values = np.where((row <= N // 2)[:, None], np.cos(angle), np.sin(angle))
    scale = np.where((row == 0) | (row == N // 2), math.sqrt(1.0 / N), math.sqrt(2.0 / N))
    return values * scale[:, None]


def profile_table():
    frequency = np.arange(N) - N // 2
    angle = angles(frequency, np.arange(N))
    return split_table(np.concatenate([np.cos(angle), np.sin(angle)]))


def packed_tables(named, exact={}):
    blocks, places, row = [], {}, 0
    for name, table in named.items():
        parts = split_table(table)
        rows, columns = parts.shape[1:]
        tall = -(-rows // 16) * 16
        block = np.zeros((2, tall, 256), ml_dtypes.bfloat16)
        block[:, :rows, :columns] = parts
        blocks.append(block.reshape(2 * tall, 256))
        places[name] = (row, row + tall, rows, columns)
        row += 2 * tall
    for name, table in exact.items():
        blocks.append(table.astype(ml_dtypes.bfloat16))
        places[name] = row
        row += table.shape[0]
    return np.concatenate(blocks), places


def holder_planes():
    holder = np.arange(N)
    return ((holder % 2) * 8 + holder // 16) * SUBS + (holder // 2) % 8


def early_tables():
    return packed_tables(
        {
            "y_inverse": y_inverse_table(),
            "x_inverse": x_inverse_table(),
            "real": real_table(),
            "real_turned": real_table().T,
        },
        {"replicate": replicate_table()},
    )


def late_tables():
    return packed_tables(
        {
            "real_planes": real_table()[:, holder_planes()],
            "planes_real": real_table().T[holder_planes()],
            "real": real_table(),
            "real_turned": real_table().T,
            "x_forward": x_forward_table(),
            "y_forward": y_forward_table(),
        },
        {"spread": spread_table()},

    )


EARLY, EARLY_PLACES = early_tables()
LATE, LATE_PLACES = late_tables()


def table_of(ref, places, name):
    high, low, rows, columns = places[name]
    return ref[high : high + rows, 0:columns], ref[low : low + rows, 0:columns]


def early_table(ref, name):
    return table_of(ref, EARLY_PLACES, name)


def late_table(ref, name):
    return table_of(ref, LATE_PLACES, name)


def halves(values):
    high = values.astype(bf16)
    return high, (values - high.astype(f32)).astype(bf16)


def dot(a, b, dims=((1,), (0,))):
    return lax.dot_general(a, b, (dims, ((), ())), preferred_element_type=f32)


def dot3(left, right, dims=((1,), (0,))):
    return dot(left[0], right[0], dims) + (dot(left[0], right[1], dims) + dot(left[1], right[0], dims))


def pair(ref):
    return ref[0], ref[1]


def stick_frequencies(columns):
    across = columns >> 7
    inplane = columns & (N - 1)
    across = jnp.where(across >= N // 2, across - N, across)
    inplane = jnp.where(inplane >= N // 2, inplane - N, inplane)
    return across, inplane


def kept_rows(shape):
    row = lax.broadcasted_iota(jnp.int32, shape, 0)
    return jnp.where(row >= 40, row + 56 - N, row)


def sphere_radius(columns):
    across, inplane = stick_frequencies(columns)
    frequency = kept_rows((LINE, columns.shape[1]))
    return frequency * frequency + (across * across + inplane * inplane)


def own_columns(columns_ref):
    group = lax.axis_index(GA_AXES)
    return jnp.concatenate([columns_ref[pl.ds(2 * group + half, 1), :] for half in range(2)], 1)


def lines_kernel(orbital_ref, tangent_ref, columns_ref, table_ref, out_ref):
    inside = sphere_radius(own_columns(columns_ref)) <= CUT * CUT
    for which, ref in enumerate((orbital_ref, tangent_ref)):
        parts = []
        for part in range(2):
            kept = jnp.concatenate([ref[0, part, 0:40, :], ref[0, part, 96:128, :]], 0)
            parts.append(jnp.where(inside, kept, 0.0))
        lines = dot3(pair(table_ref), halves(jnp.concatenate(parts, 0)))
        for part in range(2):
            for half in range(2):
                row = half * 4 + which * 2 + part
                out_ref[pl.ds(row, N, stride=8), :] = lines[part * N : (part + 1) * N, half * N : (half + 1) * N]


def circle_reach(slot):
    across = slot - CUT
    return math.isqrt(CUT * CUT - across * across) if abs(across) <= CUT else -1


def fields_kernel(
    dest_ref, lines_ref, planes_ref, tables, late_ref, fields_ref, sums_ref, late_out, turned, grid, middle, arrival
):
    del planes_ref
    copy = pltpu.make_async_copy(late_ref, late_out, arrival)
    copy.start()
    replicate = tables[EARLY_PLACES["replicate"] : EARLY_PLACES["replicate"] + 4 * N, :]
    lower = lax.broadcasted_iota(jnp.int32, (8, N), 0) < 4
    for quad in range(4):
        for half in range(2):
            tiles = []
            for group in range(4 * quad, 4 * quad + 4):
                for sub in range(0, SUBS, 2):
                    first, second = lines_ref[sub * GROUPS + group], lines_ref[(sub + 1) * GROUPS + group]
                    if half == 0:
                        tiles.append(jnp.where(lower, first, pltpu.roll(second, 4, 0)))
                    else:
                        tiles.append(jnp.where(lower, pltpu.roll(first, 4, 0), second))
            both = jnp.concatenate(halves(jnp.concatenate(tiles, 0).T), 1)
            base = (quad * 2 + half) * N
            for couple in range(2):
                copies = dot(both, replicate[couple * 2 * N : (couple + 1) * 2 * N])
                for side in range(2):
                    turned[2 * couple + side, base : base + N, :] = copies[:, side * N : (side + 1) * N]
    for quad in range(4):

        def scatter(step, carry, quad=quad):
            for inner in range(8):
                stick = step * 8 + inner
                for slot in range(4):
                    places = dest_ref[(4 * quad + slot) * N + stick]
                    grid[pl.ds(places & 0xFFFF, 1), :] = turned[slot, pl.ds(quad * 2 * N + stick, 1), :]
                    grid[pl.ds(places >> 16, 1), :] = turned[slot, pl.ds((quad * 2 + 1) * N + stick, 1), :]
            return carry

        lax.fori_loop(0, N // 8, scatter, 0)
    lane = lax.broadcasted_iota(jnp.int32, (LINE, N), 1)
    distance = jnp.abs(lax.broadcasted_iota(jnp.int32, (LINE, N), 0) - CUT)
    masks = [lane // 32 == slot for slot in range(4)]
    for step in range(17, 24):
        middle[step * PITCH : step * PITCH + N, :] = jnp.zeros((N, N), f32)
    ytable = early_table(tables, "y_inverse")
    for step in range(17):
        packed = None
        for slot in range(4):
            slab = grid[(4 * step + slot) * LINE : (4 * step + slot + 1) * LINE, :]
            packed = slab if packed is None else jnp.where(masks[slot], slab, packed)
        reach = jnp.full((1, N), circle_reach(4 * step), jnp.int32)
        for slot in range(1, 4):
            reach = jnp.where(masks[slot][0:1], circle_reach(4 * step + slot), reach)
        packed = jnp.where(distance <= reach, packed, 0.0)
        lines = dot3(halves(packed.T), ytable)
        for slot in range(4):
            real, imag = lines[slot * 32 : slot * 32 + 16], lines[slot * 32 + 16 : slot * 32 + 32]
            base = step * PITCH + slot * 16
            middle[base : base + 16, :] = real[:, 0:N] - imag[:, N : 2 * N]
            middle[base + 64 : base + 80, :] = real[:, N : 2 * N] + imag[:, 0:N]
    density = jnp.zeros((N, N), f32)
    response = jnp.zeros((N, N), f32)
    xtable = early_table(tables, "x_inverse")
    for band in range(SUBS):
        sides = []
        for which in range(2):
            rows = []
            for part in range(2):
                for slot in range(4):
                    rows.append(middle[pl.ds(part * 64 + slot * 16 + band * 2 + which, 24, stride=PITCH), :])
            sides.append(jnp.concatenate(rows, 0))
        field = dot3(xtable, halves(jnp.concatenate(sides, 1)))
        fields_ref[band] = field
        first, second = field[:, 0:N], field[:, N : 2 * N]
        density = density + first[0:N] * first[0:N] + first[N : 2 * N] * first[N : 2 * N]
        response = response + first[0:N] * second[0:N] + first[N : 2 * N] * second[N : 2 * N]
    density = density * (1.0 / BANDS)
    response = response * (2.0 / BANDS)
    spectrum = dot3(
        halves(dot3(early_table(tables, "real"), halves(response))), early_table(tables, "real_turned")
    )
    for half in range(2):
        sums_ref[pl.ds(half, 64, stride=4), :] = density[half * 64 : half * 64 + 64]
        sums_ref[pl.ds(2 + half, 64, stride=4), :] = spectrum[half * 64 : half * 64 + 64]
    copy.wait()


def mix_kernel(arrived_ref, sums_ref, spread_ref):
    for x_low in range(2):
        base = x_low * 128
        rows = [arrived_ref[base + copy * 32 : base + copy * 32 + 32, :] for copy in range(4)]
        sums_ref[x_low * 32 : x_low * 32 + 32, :] = (rows[0] + rows[1]) + (rows[2] + rows[3])
    spectrum = [sums_ref[pl.ds(2 + half, 16, stride=4), :] for half in range(2)]
    for copy in range(8):
        for half in range(2):
            base = copy * 32 + half * 16
            spread_ref[base : base + 16, :] = spectrum[half]


def hartree_kernel(sums_ref, columns_ref, tables_ref, out_ref):
    sides = []
    for half in range(2):
        sides.append(jnp.concatenate([columns_ref[z * 32 + half * 16 : z * 32 + half * 16 + 16, :] for z in range(8)], 0))
    lines = dot3(late_table(tables_ref, "real_planes"), halves(jnp.concatenate(sides, 1)))
    shape = (N, 2 * N)
    row = lax.broadcasted_iota(jnp.int32, shape, 0)
    lane = lax.broadcasted_iota(jnp.int32, shape, 1)
    across = lax.axis_index(BAND_AXES) * 2 + lax.axis_index("xh") + jnp.where(lane >= N, 64, 0)
    inplane = lane & (N - 1)

    def frequency(index):
        return jnp.where(index <= N // 2, index, index - N // 2)

    across, inplane, row = frequency(across), frequency(inplane), frequency(row)
    squares = (row * row + across * across + inplane * inplane).astype(f32)
    kernel = jnp.where(squares == 0.0, 0.0, (4.0 * math.pi / FACTOR) / jnp.where(squares == 0.0, 1.0, squares))
    back = dot3(late_table(tables_ref, "planes_real"), halves(lines * kernel))
    own = lax.axis_index("z")
    mine = back[0:16]
    for z in range(1, 8):
        mine = jnp.where(own == z, back[z * 16 : z * 16 + 16], mine)
    back = mine
    for half in range(2):
        fields = [
            back[:, half * N : (half + 1) * N],
            sums_ref[pl.ds(half, 16, stride=4), :],
            sums_ref[pl.ds(2 + half, 16, stride=4), :],
        ]
        for which, field in enumerate(fields):
            for x_low in range(2):
                for copy in range(4):
                    base = (x_low * 32 + copy * 8) * 6 + which * 2 + half
                    out_ref[pl.ds(base, 8, stride=6), :] = field[x_low * 8 : x_low * 8 + 8]


def own_plane():
    return lax.axis_index(GA_AXES) * SUBS + lax.axis_index(("xl", "yl", "core"))


def ions_kernel(
    atom_ref,
    direction_ref,
    positions_ref,
    charge_ref,
    widths_ref,
    table_ref,
    potential_ref,
    core_ref,
    out_ref,
    centres,
    spreads,
    marks,
    charges,
    arrivals,
):
    own = lax.axis_index(("xl", "yl", "core"))
    copies = [
        pltpu.make_async_copy(potential_ref.at[own], out_ref.at[0], arrivals.at[0]),
        pltpu.make_async_copy(core_ref.at[own], out_ref.at[1], arrivals.at[1]),
    ]
    for copy in copies:
        copy.start()
    for slot in range(DISP):
        atom = atom_ref[slot]
        charges[slot : slot + 1, :] = jnp.full((1, N), charge_ref[atom] * (-1.0 / CELL), f32)
        for axis in range(3):
            row = axis * DISP + slot
            centres[row : row + 1, :] = jnp.full((1, N), positions_ref[axis, atom], f32)
            spreads[row : row + 1, :] = jnp.full((1, N), widths_ref[atom], f32)
            marks[row : row + 1, :] = jnp.full((1, N), jnp.where(direction_ref[slot] == axis, 1.0, 0.0), f32)
    frequency = lax.broadcasted_iota(jnp.int32, (3 * DISP, N), 1) - N // 2
    wavenum = frequency.astype(f32) * (2.0 * math.pi / CELL)
    damping = jnp.exp(-0.5 * (wavenum * spreads[...]) ** 2)
    phase = wavenum * centres[...]
    cosine, sine = damping * jnp.cos(phase), damping * jnp.sin(phase)
    chosen = marks[...] > 0.5
    with_cos = jnp.where(chosen, -wavenum * sine, cosine)
    with_sin = jnp.where(chosen, wavenum * cosine, sine)
    profiles = dot3(halves(jnp.concatenate([with_cos, with_sin], 1)), pair(table_ref))
    along_x, along_y, along_z = profiles[0:8], profiles[8:16], profiles[16:24]
    lane = lax.broadcasted_iota(jnp.int32, (DISP, N), 1)
    here = jnp.sum(jnp.where(lane == own_plane(), along_z, 0.0), 1, keepdims=True)
    scaled = along_y * here * charges[...]
    padding = jnp.zeros((N - DISP, N), f32)
    left = jnp.concatenate([along_x, padding], 0).T
    right = jnp.concatenate([scaled, padding], 0)
    out_ref[2] = dot3(halves(left), halves(right))
    for copy in copies:
        copy.wait()


def products_kernel(
    dest_ref,
    fields_ref,
    solved_ref,
    planes_ref,
    tables_ref,
    out_ref,
    lines,
    grid,
    gathered,
):
    def solved(which):
        return jnp.concatenate([solved_ref[pl.ds(which * 2 + half, 64, stride=6), :] for half in range(2)], 0)

    waves = dot3(late_table(tables_ref, "real_turned"), halves(jnp.concatenate([solved(0), solved(2)], 1)))
    waves = dot3(halves(jnp.concatenate([waves[:, 0:N], waves[:, N : 2 * N]], 0)), late_table(tables_ref, "real"))
    hartree, response = waves[0:N], waves[N : 2 * N]
    total = solved(1) + planes_ref[1]
    root = jnp.exp(jnp.log(total) * (1.0 / 3.0))
    exchange = -SLATER * root
    effective = planes_ref[0] + exchange
    change = exchange / (3.0 * total) * response + hartree + planes_ref[2]
    xtable = late_table(tables_ref, "x_forward")
    ytable = late_table(tables_ref, "y_forward")
    effective2 = jnp.concatenate([effective, effective], 0)
    change2 = jnp.concatenate([change, change], 0)
    blocks = [[], []]
    for couple in range(SUBS // 2):
        sides = []
        for band in (2 * couple, 2 * couple + 1):
            sides.append(effective2 * fields_ref[band, :, N : 2 * N] + change2 * fields_ref[band, :, 0:N])
        across = dot3(xtable, halves(jnp.concatenate(sides, 1)))
        rows = jnp.concatenate([across[:, 0:N], across[:, N : 2 * N]], 0)
        done = dot3(halves(rows), ytable)
        for side in range(2):
            real = done[side * 144 : side * 144 + 72]
            imag = done[side * 144 + 72 : side * 144 + 144]
            base = (2 * couple + side) * 144
            lines[base : base + 72, :] = real[:, 0:N] + imag[:, N : 2 * N]
            lines[base + 72 : base + 144, :] = imag[:, 0:N] - real[:, N : 2 * N]
    first = LATE_PLACES["spread"]
    spread = [tables_ref[first + block * 2 * N : first + (block + 1) * 2 * N, :] for block in range(4)]
    for eight in range(9):
        tiles = [lines[half * 72 + eight * 8 : half * 72 + eight * 8 + 8, :] for half in range(16)]
        turned = jnp.concatenate(tiles, 0).T[0:LINE]
        high, low = halves(turned)
        both = jnp.concatenate([high, low], 1)
        for block in range(4):
            cells = dot(both, spread[block])
            for side in range(2):
                base = (eight * 8 + block * 2 + side) * LINE
                grid[base : base + LINE, :] = cells[:, side * N : (side + 1) * N]
    lane = lax.broadcasted_iota(jnp.int32, (1, N), 1)
    slot_of_lane = ((lane // 4) % 4) * 2 + lane % 2
    masks = [slot_of_lane == slot for slot in range(1, 8)]
    for block in range(4):

        def gather(step, carry, block=block):
            for inner in range(8):
                stick = step * 8 + inner
                row = None
                for slot in range(4):
                    places = dest_ref[(4 * block + slot) * N + stick]
                    cells = [grid[pl.ds(places & 0xFFFF, 1), :], grid[pl.ds(places >> 16, 1), :]]
                    for half in range(2):
                        row = cells[half] if row is None else jnp.where(masks[2 * slot + half - 1], cells[half], row)
                gathered[pl.ds(stick, 1), :] = row
            return carry

        lax.fori_loop(0, N // 8, gather, 0)
        turned = gathered[...].T
        for band in range(SUBS):
            base = band * 64 + block * 16
            out_ref[base : base + 16, :] = turned[band * 16 : band * 16 + 16]


def result_kernel(arrived_ref, tangent_ref, columns_ref, table_ref, out_ref):
    sides = []
    for half in range(2):
        parts = [arrived_ref[pl.ds(part * 2 + half, N, stride=4), :] for part in range(2)]
        sides.append(jnp.concatenate(parts, 0))
    lines = dot3(pair(table_ref), halves(jnp.concatenate(sides, 1)))
    radius = sphere_radius(own_columns(columns_ref))
    inside = radius <= CUT * CUT
    kinetic = (0.5 * FACTOR) * radius.astype(f32)
    for part in range(2):
        kept = jnp.concatenate([tangent_ref[0, part, 0:40, :], tangent_ref[0, part, 96:128, :]], 0)
        rows = jnp.where(inside, lines[part * LINE : (part + 1) * LINE] + kinetic * kept, 0.0)
        out_ref[0, part, 0:40, :] = rows[0:40]
        out_ref[0, part, 40:96, :] = jnp.zeros((56, 256), f32)
        out_ref[0, part, 96:128, :] = rows[40:72]


def vmem(count):
    return [pl.BlockSpec(memory_space=pltpu.VMEM)] * count


def anywhere(count):
    return [pl.BlockSpec(memory_space=pltpu.HBM)] * count


def smem(count):
    return [pl.BlockSpec(memory_space=pltpu.SMEM)] * count


def shape(*dims):
    return jax.ShapeDtypeStruct(dims, f32)


def call(kernel, out_shape, in_specs, mebibytes, scratch=()):
    several = isinstance(out_shape, tuple)
    return pl.pallas_call(
        kernel,
        out_shape=out_shape,
        in_specs=in_specs,
        out_specs=tuple(vmem(len(out_shape))) if several else vmem(1)[0],
        scratch_shapes=scratch,
        compiler_params=pltpu.CompilerParams(vmem_limit_bytes=(mebibytes << 20) or None),
        name=kernel.__name__.removesuffix("_kernel"),
    )


def exchange(values, axes):
    return lax.all_to_all(values, axes, 0, 0, tiled=True)


def body(
    orbitals,
    orbital_tangent,
    stick_columns,
    ion_potential,
    core_density,
    positions,
    z_charge,
    widths,
    atom_index,
    direction,
):
    columns = stick_columns.reshape(STICKS // N, N)
    across, inplane = stick_frequencies(stick_columns)
    cell = (across + CUT) * LINE + (inplane + CUT)
    dest = jnp.where(across * across + inplane * inplane <= CUT * CUT, cell, DUMP).reshape(GROUPS, 2, N)
    dest = (dest[:, 0] + dest[:, 1] * 65536).reshape(-1)
    lines = call(lines_kernel, shape(N * 8, N), vmem(4), 0)(orbitals, orbital_tangent, columns, z_inverse_table())
    lines = exchange(lines.reshape(N, 8, N), PLANE_AXES)
    planes = call(
        ions_kernel,
        shape(3, N, N),
        smem(5) + vmem(1) + anywhere(2),
        4,
        [pltpu.VMEM((24, N), f32)] * 3 + [pltpu.VMEM((8, N), f32), pltpu.SemaphoreType.DMA((2,))],
    )(atom_index, direction, positions.T, z_charge, widths, profile_table(), ion_potential, core_density)
    fields, sums, tables = call(
        fields_kernel,
        (shape(SUBS, 2 * N, 2 * N), shape(2 * N, N), jax.ShapeDtypeStruct(LATE.shape, bf16)),
        smem(1) + vmem(1) + anywhere(1) + vmem(1) + anywhere(1),
        24,
        [
            pltpu.VMEM((4, 8 * N, N), f32),
            pltpu.VMEM((CELLS, N), f32),
            pltpu.VMEM((24 * PITCH, N), f32),
            pltpu.SemaphoreType.DMA,
        ],
    )(dest, lines, planes, EARLY, LATE)
    sums = exchange(sums.reshape(64, 4, N), BAND_AXES + ("xh",)).reshape(2 * N, N)
    sums, spectrum = call(mix_kernel, (shape(64, N), shape(2 * N, N)), vmem(1), 4)(sums)
    spectrum = exchange(spectrum.reshape(8, 32, N), "z").reshape(2 * N, N)
    solved = call(hartree_kernel, shape(3 * N, N), vmem(3), 4)(sums, spectrum, tables)
    solved = exchange(solved.reshape(64, 3, 2, N), BAND_AXES + ("xh",)).reshape(3 * N, N)
    outgoing = call(
        products_kernel,
        shape(4 * N, N),
        smem(1) + vmem(4),
        20,
        [
            pltpu.VMEM((16 * LINE, N), f32),
            pltpu.VMEM((LINE * LINE, N), f32),
            pltpu.VMEM((N, N), f32),
        ],
    )(
        dest,
        fields,
        solved,
        planes,
        tables,
    )
    arrived = exchange(outgoing.reshape(N, 4, N), PLANE_AXES).reshape(4 * N, N)
    return call(result_kernel, shape(1, 2, N, 256), vmem(4), 8)(arrived, orbital_tangent, columns, z_forward_table())


def solution(mesh):
    fine = Mesh(mesh.devices.reshape(2, 4, 2, 2, 2, 8), BAND_AXES + GA_AXES)
    lines = P(BAND_AXES, None, None, GA_AXES)
    planes = P(GA_AXES, None, None)
    return jax.shard_map(
        body,
        mesh=fine,
        in_specs=(lines, lines, P(), planes, planes, P(), P(), P(), P(), P()),
        out_specs=lines,
        check_vma=False,
    )
```

```python
import functools
import math

import jax
import jax.numpy as jnp
import ml_dtypes
import numpy as np
from jax import lax
from jax.experimental import pallas as pl
from jax.experimental.pallas import tpu as pltpu
from jax.sharding import Mesh, PartitionSpec as P

N = 128
BANDS = 32
STICKS = 4096
DISP = 8
CUT = N // 4
LINE = 72
SLABS = 68
CELLS = SLABS * LINE
PAIRS = 40
TURNED_ROW = PAIRS + CUT
DUMP = 65 * LINE
CELL = 40.0
SLATER = (3.0 / math.pi) ** (1.0 / 3.0)
FACTOR = (2.0 * math.pi / CELL) ** 2
WEIGHT = 4.0 / N**1.5

BAND_AXES = ("xl", "yh", "yl", "core")
GA_AXES = ("xh", "z")
PLANE_AXES = ("xl", "yl", "core", "xh", "z")
SUBS = 8
PITCH = 136
GROUPS = 16

f32 = jnp.float32
bf16 = jnp.bfloat16


def split_table(table):
    table = np.asarray(table, np.float64)
    high = table.astype(np.float32).astype(ml_dtypes.bfloat16)
    low = (table - high.astype(np.float64)).astype(np.float32).astype(ml_dtypes.bfloat16)
    return np.stack([high, low])


def signed(values):
    return np.where(values >= N // 2, values - N, values)


def angles(rows, columns):
    return 2.0 * np.pi * (np.outer(rows, columns) % N) / N


def plane_of_holder():
    holder = np.arange(N)
    return (holder % GROUPS) * SUBS + holder // GROUPS


def z_inverse_table():
    kept = np.concatenate([np.arange(0, 40), np.arange(96, 128)])
    angle = angles(plane_of_holder(), kept)
    inside = np.abs(signed(kept)) <= CUT
    cosine, sine = np.cos(angle) * inside, np.sin(angle) * inside
    return split_table(np.block([[cosine, -sine], [sine, cosine]]))


def z_forward_table():
    kept = np.concatenate([np.arange(0, 40), np.arange(96, 128)])
    angle = angles(kept, plane_of_holder())
    scale = 1.0 / (WEIGHT * N**3)
    cosine, sine = np.cos(angle) * scale, np.sin(angle) * scale
    return split_table(np.block([[cosine, sine], [-sine, cosine]]))


def box_frequencies(count):
    slot = np.arange(count)
    return slot - CUT, (slot <= 2 * CUT).astype(np.float64)


def y_inverse_table():
    frequency, kept = box_frequencies(LINE)
    angle = angles(frequency, np.arange(N))
    return (np.concatenate([np.cos(angle), np.sin(angle)], 1) * kept[:, None])


def x_inverse_table():
    across = (4 * np.arange(24)[None, :] + np.arange(4)[:, None]).reshape(-1)
    kept = (across <= 2 * CUT).astype(np.float64)
    angle = angles(np.arange(N), across - CUT)
    cosine, sine = WEIGHT * np.cos(angle) * kept, WEIGHT * np.sin(angle) * kept
    return (np.block([[cosine, -sine], [sine, cosine]]))


def x_forward_table():
    slot = np.concatenate([2 * np.arange(40), 2 * np.arange(40) + 1])
    kept = (slot <= 2 * CUT).astype(np.float64)
    angle = angles(slot - CUT, np.arange(N))
    cosine, sine = np.cos(angle) * kept[:, None], np.sin(angle) * kept[:, None]
    real, imag = np.concatenate([cosine, sine], 1), np.concatenate([-sine, cosine], 1)
    real[TURNED_ROW, :N] = 1.0
    imag[TURNED_ROW, N:] = -1.0
    return np.concatenate([real, imag])


def y_forward_table():
    lane = np.arange(N) % 64
    angle = angles(np.arange(N), np.where(lane <= CUT, lane, lane - 64))
    return np.concatenate([np.cos(angle), np.sin(angle)], 1)


def replicate_table():
    table = np.zeros((N, 4, 4, 2, 16))
    for group in range(4):
        for part in range(2):
            for entry in range(16):
                table[group * 32 + entry * 2 + part, group, :, part, entry] = 1.0
    table = table.reshape(N, 2, 2 * N).transpose(1, 0, 2)
    return np.concatenate([table, table], 1).reshape(4 * N, 2 * N)


def real_table():
    row = np.arange(N)
    frequency = np.where(row <= N // 2, row, row - N // 2)
    angle = angles(frequency, np.arange(N))
    values = np.where((row <= N // 2)[:, None], np.cos(angle), np.sin(angle))
    scale = np.where((row == 0) | (row == N // 2), math.sqrt(1.0 / N), math.sqrt(2.0 / N))
    return values * scale[:, None]


def profile_table():
    frequency = np.arange(N) - N // 2
    angle = angles(frequency, np.arange(N))
    return split_table(np.concatenate([np.cos(angle), np.sin(angle)]))


def packed_tables(named, exact={}):
    blocks, places, row = [], {}, 0
    for name, table in named.items():
        parts = split_table(table)
        rows, columns = parts.shape[1:]
        tall = -(-rows // 16) * 16
        block = np.zeros((2, tall, 256), ml_dtypes.bfloat16)
        block[:, :rows, :columns] = parts
        blocks.append(block.reshape(2 * tall, 256))
        places[name] = (row, row + tall, rows, columns)
        row += 2 * tall
    for name, table in exact.items():
        blocks.append(table.astype(ml_dtypes.bfloat16))
        places[name] = row
        row += table.shape[0]
    return np.concatenate(blocks), places


def holder_planes():
    holder = np.arange(N)
    return ((holder % 2) * 8 + holder // 16) * SUBS + (holder // 2) % 8


def early_tables():
    return packed_tables(
        {
            "y_inverse": y_inverse_table(),
            "x_inverse": x_inverse_table(),
            "real": real_table(),
            "real_turned": real_table().T,
        },
        {"replicate": replicate_table()},
    )


def late_tables():
    return packed_tables(
        {
            "real_planes": real_table()[:, holder_planes()],
            "planes_real": real_table().T[holder_planes()],
            "real": real_table(),
            "real_turned": real_table().T,
            "x_forward": x_forward_table(),
            "y_forward": y_forward_table(),
        }

    )


EARLY, EARLY_PLACES = early_tables()
LATE, LATE_PLACES = late_tables()


def table_of(ref, places, name):
    high, low, rows, columns = places[name]
    tall = low - high
    return ref[high : high + tall, 0:columns][0:rows], ref[low : low + tall, 0:columns][0:rows]


def early_table(ref, name):
    return table_of(ref, EARLY_PLACES, name)


def late_table(ref, name):
    return table_of(ref, LATE_PLACES, name)


def halves(values):
    high = values.astype(bf16)
    return high, (values - high.astype(f32)).astype(bf16)


def dot(a, b, dims=((1,), (0,))):
    return lax.dot_general(a, b, (dims, ((), ())), preferred_element_type=f32)


def dot3(left, right, dims=((1,), (0,))):
    return dot(left[0], right[0], dims) + (dot(left[0], right[1], dims) + dot(left[1], right[0], dims))


def pair(ref):
    return ref[0], ref[1]


def stick_frequencies(columns):
    across = columns >> 7
    inplane = columns & (N - 1)
    across = jnp.where(across >= N // 2, across - N, across)
    inplane = jnp.where(inplane >= N // 2, inplane - N, inplane)
    return across, inplane


def kept_rows(shape):
    row = lax.broadcasted_iota(jnp.int32, shape, 0)
    return jnp.where(row >= 40, row + 56 - N, row)


def sphere_radius(columns):
    across, inplane = stick_frequencies(columns)
    frequency = kept_rows((LINE, columns.shape[1]))
    return frequency * frequency + (across * across + inplane * inplane)


def own_columns(columns_ref):
    group = lax.axis_index(GA_AXES)
    return jnp.concatenate([columns_ref[pl.ds(2 * group + half, 1), :] for half in range(2)], 1)


def lines_kernel(orbital_ref, tangent_ref, columns_ref, table_ref, out_ref):
    inside = sphere_radius(own_columns(columns_ref)) <= CUT * CUT
    for which, ref in enumerate((orbital_ref, tangent_ref)):
        parts = []
        for part in range(2):
            kept = jnp.concatenate([ref[0, part, 0:40, :], ref[0, part, 96:128, :]], 0)
            parts.append(jnp.where(inside, kept, 0.0))
        lines = dot3(pair(table_ref), halves(jnp.concatenate(parts, 0)))
        for part in range(2):
            for half in range(2):
                row = half * 4 + which * 2 + part
                out_ref[pl.ds(row, N, stride=8), :] = lines[part * N : (part + 1) * N, half * N : (half + 1) * N]


def circle_reach(slot):
    across = slot - CUT
    return math.isqrt(CUT * CUT - across * across) if abs(across) <= CUT else -1


def fields_kernel(
    dest_ref, lines_ref, tables, fields_ref, sums_ref, turned, grid, middle
):
    replicate = tables[EARLY_PLACES["replicate"] : EARLY_PLACES["replicate"] + 4 * N, :]
    lower = lax.broadcasted_iota(jnp.int32, (8, N), 0) < 4
    for quad in range(4):
        for half in range(2):
            tiles = []
            for group in range(4 * quad, 4 * quad + 4):
                for sub in range(0, SUBS, 2):
                    first, second = lines_ref[sub * GROUPS + group], lines_ref[(sub + 1) * GROUPS + group]
                    if half == 0:
                        tiles.append(jnp.where(lower, first, pltpu.roll(second, 4, 0)))
                    else:
                        tiles.append(jnp.where(lower, pltpu.roll(first, 4, 0), second))
            both = jnp.concatenate(halves(jnp.concatenate(tiles, 0).T), 1)
            base = (quad * 2 + half) * N
            for couple in range(2):
                copies = dot(both, replicate[couple * 2 * N : (couple + 1) * 2 * N])
                for side in range(2):
                    turned[2 * couple + side, base : base + N, :] = copies[:, side * N : (side + 1) * N]
    for quad in range(4):

        def scatter(step, carry, quad=quad):
            for inner in range(8):
                stick = step * 8 + inner
                for slot in range(4):
                    places = dest_ref[(4 * quad + slot) * N + stick]
                    grid[pl.ds(places & 0xFFFF, 1), :] = turned[slot, pl.ds(quad * 2 * N + stick, 1), :]
                    grid[pl.ds(places >> 16, 1), :] = turned[slot, pl.ds((quad * 2 + 1) * N + stick, 1), :]
            return carry

        lax.fori_loop(0, N // 8, scatter, 0)
    lane = lax.broadcasted_iota(jnp.int32, (LINE, N), 1)
    distance = jnp.abs(lax.broadcasted_iota(jnp.int32, (LINE, N), 0) - CUT)
    masks = [lane // 32 == slot for slot in range(4)]
    for step in range(17, 24):
        middle[step * PITCH : step * PITCH + N, :] = jnp.zeros((N, N), f32)
    ytable = early_table(tables, "y_inverse")
    for step in range(17):
        packed = None
        for slot in range(4):
            slab = grid[(4 * step + slot) * LINE : (4 * step + slot + 1) * LINE, :]
            packed = slab if packed is None else jnp.where(masks[slot], slab, packed)
        reach = jnp.full((1, N), circle_reach(4 * step), jnp.int32)
        for slot in range(1, 4):
            reach = jnp.where(masks[slot][0:1], circle_reach(4 * step + slot), reach)
        packed = jnp.where(distance <= reach, packed, 0.0)
        lines = dot3(halves(packed.T), ytable)
        for slot in range(4):
            real, imag = lines[slot * 32 : slot * 32 + 16], lines[slot * 32 + 16 : slot * 32 + 32]
            base = step * PITCH + slot * 16
            middle[base : base + 16, :] = real[:, 0:N] - imag[:, N : 2 * N]
            middle[base + 64 : base + 80, :] = real[:, N : 2 * N] + imag[:, 0:N]
    density = jnp.zeros((N, N), f32)
    response = jnp.zeros((N, N), f32)
    xtable = early_table(tables, "x_inverse")
    for band in range(SUBS):
        sides = []
        for which in range(2):
            rows = []
            for part in range(2):
                for slot in range(4):
                    rows.append(middle[pl.ds(part * 64 + slot * 16 + band * 2 + which, 24, stride=PITCH), :])
            sides.append(jnp.concatenate(rows, 0))
        field = dot3(xtable, halves(jnp.concatenate(sides, 1)))
        fields_ref[band] = field
        first, second = field[:, 0:N], field[:, N : 2 * N]
        density = density + first[0:N] * first[0:N] + first[N : 2 * N] * first[N : 2 * N]
        response = response + first[0:N] * second[0:N] + first[N : 2 * N] * second[N : 2 * N]
    density = density * (1.0 / BANDS)
    response = response * (2.0 / BANDS)
    spectrum = dot3(
        halves(dot3(early_table(tables, "real"), halves(response))), early_table(tables, "real_turned")
    )
    for half in range(2):
        sums_ref[pl.ds(half, 64, stride=4), :] = density[half * 64 : half * 64 + 64]
        sums_ref[pl.ds(2 + half, 64, stride=4), :] = spectrum[half * 64 : half * 64 + 64]


def mix_kernel(arrived_ref, sums_ref, spread_ref):
    for x_low in range(2):
        base = x_low * 128
        rows = [arrived_ref[base + copy * 32 : base + copy * 32 + 32, :] for copy in range(4)]
        sums_ref[x_low * 32 : x_low * 32 + 32, :] = (rows[0] + rows[1]) + (rows[2] + rows[3])
    spectrum = [sums_ref[pl.ds(2 + half, 16, stride=4), :] for half in range(2)]
    for copy in range(8):
        for half in range(2):
            base = copy * 32 + half * 16
            spread_ref[base : base + 16, :] = spectrum[half]


def hartree_kernel(sums_ref, columns_ref, tables_ref, out_ref):
    sides = []
    for half in range(2):
        sides.append(jnp.concatenate([columns_ref[z * 32 + half * 16 : z * 32 + half * 16 + 16, :] for z in range(8)], 0))
    lines = dot3(late_table(tables_ref, "real_planes"), halves(jnp.concatenate(sides, 1)))
    shape = (N, 2 * N)
    row = lax.broadcasted_iota(jnp.int32, shape, 0)
    lane = lax.broadcasted_iota(jnp.int32, shape, 1)
    across = lax.axis_index(BAND_AXES) * 2 + lax.axis_index("xh") + jnp.where(lane >= N, 64, 0)
    inplane = lane & (N - 1)

    def frequency(index):
        return jnp.where(index <= N // 2, index, index - N // 2)

    across, inplane, row = frequency(across), frequency(inplane), frequency(row)
    squares = (row * row + across * across + inplane * inplane).astype(f32)
    kernel = jnp.where(squares == 0.0, 0.0, (4.0 * math.pi / FACTOR) / jnp.where(squares == 0.0, 1.0, squares))
    back = dot3(late_table(tables_ref, "planes_real"), halves(lines * kernel))
    own = lax.axis_index("z")
    mine = back[0:16]
    for z in range(1, 8):
        mine = jnp.where(own == z, back[z * 16 : z * 16 + 16], mine)
    back = mine
    for half in range(2):
        fields = [
            back[:, half * N : (half + 1) * N],
            sums_ref[pl.ds(half, 16, stride=4), :],
            sums_ref[pl.ds(2 + half, 16, stride=4), :],
        ]
        for which, field in enumerate(fields):
            for x_low in range(2):
                for copy in range(4):
                    base = (x_low * 32 + copy * 8) * 6 + which * 2 + half
                    out_ref[pl.ds(base, 8, stride=6), :] = field[x_low * 8 : x_low * 8 + 8]


def own_plane():
    return lax.axis_index(GA_AXES) * SUBS + lax.axis_index(("xl", "yl", "core"))


def ions_kernel(
    atom_ref,
    direction_ref,
    positions_ref,
    charge_ref,
    widths_ref,
    table_ref,
    potential_ref,
    core_ref,
    early_ref,
    late_ref,
    lines_ref,
    out_ref,
    early_out,
    late_out,
    centres,
    spreads,
    marks,
    charges,
    arrivals,
):
    del lines_ref
    own = lax.axis_index(("xl", "yl", "core"))
    copies = [
        pltpu.make_async_copy(potential_ref.at[own], out_ref.at[0], arrivals.at[0]),
        pltpu.make_async_copy(core_ref.at[own], out_ref.at[1], arrivals.at[1]),
        pltpu.make_async_copy(early_ref, early_out, arrivals.at[2]),
        pltpu.make_async_copy(late_ref, late_out, arrivals.at[3]),
    ]
    for copy in copies:
        copy.start()
    for slot in range(DISP):
        atom = atom_ref[slot]
        charges[slot : slot + 1, :] = jnp.full((1, N), charge_ref[atom] * (-1.0 / CELL), f32)
        for axis in range(3):
            row = axis * DISP + slot
            centres[row : row + 1, :] = jnp.full((1, N), positions_ref[axis, atom], f32)
            spreads[row : row + 1, :] = jnp.full((1, N), widths_ref[atom], f32)
            marks[row : row + 1, :] = jnp.full((1, N), jnp.where(direction_ref[slot] == axis, 1.0, 0.0), f32)
    frequency = lax.broadcasted_iota(jnp.int32, (3 * DISP, N), 1) - N // 2
    wavenum = frequency.astype(f32) * (2.0 * math.pi / CELL)
    damping = jnp.exp(-0.5 * (wavenum * spreads[...]) ** 2)
    phase = wavenum * centres[...]
    cosine, sine = damping * jnp.cos(phase), damping * jnp.sin(phase)
    chosen = marks[...] > 0.5
    with_cos = jnp.where(chosen, -wavenum * sine, cosine)
    with_sin = jnp.where(chosen, wavenum * cosine, sine)
    profiles = dot3(halves(jnp.concatenate([with_cos, with_sin], 1)), pair(table_ref))
    along_x, along_y, along_z = profiles[0:8], profiles[8:16], profiles[16:24]
    lane = lax.broadcasted_iota(jnp.int32, (DISP, N), 1)
    here = jnp.sum(jnp.where(lane == own_plane(), along_z, 0.0), 1, keepdims=True)
    scaled = along_y * here * charges[...]
    padding = jnp.zeros((N - DISP, N), f32)
    left = jnp.concatenate([along_x, padding], 0).T
    right = jnp.concatenate([scaled, padding], 0)
    out_ref[2] = dot3(halves(left), halves(right))
    for copy in copies:
        copy.wait()


def products_kernel(columns_ref, fields_ref, solved_ref, planes_ref, tables_ref, out_ref, lines):
    def solved(which):
        return jnp.concatenate([solved_ref[pl.ds(which * 2 + half, 64, stride=6), :] for half in range(2)], 0)

    waves = dot3(late_table(tables_ref, "real_turned"), halves(jnp.concatenate([solved(0), solved(2)], 1)))
    waves = dot3(halves(jnp.concatenate([waves[:, 0:N], waves[:, N : 2 * N]], 0)), late_table(tables_ref, "real"))
    hartree, response = waves[0:N], waves[N : 2 * N]
    total = solved(1) + planes_ref[1]
    root = jnp.exp(jnp.log(total) * (1.0 / 3.0))
    exchange = -SLATER * root
    effective = planes_ref[0] + exchange
    change = exchange / (3.0 * total) * response + hartree + planes_ref[2]
    xtable = late_table(tables_ref, "x_forward")
    ytable = late_table(tables_ref, "y_forward")
    effective2 = jnp.concatenate([effective, effective], 0)
    change2 = jnp.concatenate([change, change], 0)
    lower = lax.broadcasted_iota(jnp.int32, (PAIRS, N), 1) < 64
    for couple in range(SUBS // 2):
        sides = []
        for band in (2 * couple, 2 * couple + 1):
            sides.append(effective2 * fields_ref[band, :, N : 2 * N] + change2 * fields_ref[band, :, 0:N])
        across = dot3(xtable, halves(jnp.concatenate(sides, 1)))
        rows = jnp.concatenate([across[:, 0:N], across[:, N : 2 * N]], 0)
        done = dot3(halves(rows), ytable)
        for side in range(2):
            real = done[side * 4 * PAIRS : side * 4 * PAIRS + 2 * PAIRS]
            imag = done[side * 4 * PAIRS + 2 * PAIRS : (side + 1) * 4 * PAIRS]
            whole = (real[:, 0:N] + imag[:, N : 2 * N], imag[:, 0:N] - real[:, N : 2 * N])
            for part in range(2):
                base = (part * SUBS + 2 * couple + side) * PAIRS
                lines[base : base + PAIRS, :] = jnp.where(lower, whole[part][0:PAIRS], whole[part][PAIRS : 2 * PAIRS])
    across, inplane = stick_frequencies(columns_ref[...])
    box = across + CUT
    special = jnp.logical_and(across == 0, inplane == -CUT)
    place = jnp.where(special, 64 + CUT, (box & 1) * 64 + (inplane & 63))
    held = jnp.where(special, CUT, box >> 1)
    held = jnp.where(across * across + inplane * inplane <= CUT * CUT, held, -1)
    sign = jnp.where(special, -1.0, 1.0)
    for vector in range(2 * GROUPS):
        index = jnp.broadcast_to(place[vector : vector + 1], (SUBS, N))
        wanted = jnp.broadcast_to(held[vector : vector + 1], (SUBS, N))
        picked = [jnp.zeros((SUBS, N), f32)] * 2
        for couple in range(CUT + 1):
            mask = wanted == couple
            for part in range(2):
                cells = lines[pl.ds(part * SUBS * PAIRS + couple, SUBS, stride=PAIRS), :]
                picked[part] = jnp.where(mask, jnp.take_along_axis(cells, index, axis=1), picked[part])
        picked[1] = picked[1] * sign[vector : vector + 1]
        for part in range(2):
            row = (vector // 2) * 4 + part * 2 + vector % 2
            out_ref[pl.ds(row, SUBS, stride=64), :] = picked[part]


def result_kernel(arrived_ref, tangent_ref, columns_ref, table_ref, out_ref):
    sides = []
    for half in range(2):
        parts = [arrived_ref[pl.ds(part * 2 + half, N, stride=4), :] for part in range(2)]
        sides.append(jnp.concatenate(parts, 0))
    lines = dot3(pair(table_ref), halves(jnp.concatenate(sides, 1)))
    radius = sphere_radius(own_columns(columns_ref))
    inside = radius <= CUT * CUT
    kinetic = (0.5 * FACTOR) * radius.astype(f32)
    for part in range(2):
        kept = jnp.concatenate([tangent_ref[0, part, 0:40, :], tangent_ref[0, part, 96:128, :]], 0)
        rows = jnp.where(inside, lines[part * LINE : (part + 1) * LINE] + kinetic * kept, 0.0)
        out_ref[0, part, 0:40, :] = rows[0:40]
        out_ref[0, part, 40:96, :] = jnp.zeros((56, 256), f32)
        out_ref[0, part, 96:128, :] = rows[40:72]


def vmem(count):
    return [pl.BlockSpec(memory_space=pltpu.VMEM)] * count


def anywhere(count):
    return [pl.BlockSpec(memory_space=pltpu.HBM)] * count


def smem(count):
    return [pl.BlockSpec(memory_space=pltpu.SMEM)] * count


def shape(*dims):
    return jax.ShapeDtypeStruct(dims, f32)


def call(kernel, out_shape, in_specs, mebibytes, scratch=()):
    several = isinstance(out_shape, tuple)
    return pl.pallas_call(
        kernel,
        out_shape=out_shape,
        in_specs=in_specs,
        out_specs=tuple(vmem(len(out_shape))) if several else vmem(1)[0],
        scratch_shapes=scratch,
        compiler_params=pltpu.CompilerParams(vmem_limit_bytes=(mebibytes << 20) or None),
        name=kernel.__name__.removesuffix("_kernel"),
    )


def stay(values):
    return pltpu.with_memory_space_constraint(jnp.asarray(values), pltpu.HBM)


def exchange(values, axes):
    return lax.all_to_all(values, axes, 0, 0, tiled=True)


def body(
    orbitals,
    orbital_tangent,
    stick_columns,
    ion_potential,
    core_density,
    positions,
    z_charge,
    widths,
    atom_index,
    direction,
):
    columns = stick_columns.reshape(STICKS // N, N)
    across, inplane = stick_frequencies(stick_columns)
    cell = (across + CUT) * LINE + (inplane + CUT)
    dest = jnp.where(across * across + inplane * inplane <= CUT * CUT, cell, DUMP).reshape(GROUPS, 2, N)
    dest = (dest[:, 0] + dest[:, 1] * 65536).reshape(-1)
    lines = call(lines_kernel, pltpu.VMEM((N * 8, N), f32), vmem(4), 8)(
        stay(orbitals), stay(orbital_tangent), stay(columns), stay(z_inverse_table())
    )
    arrived = exchange(lines.reshape(N, 8, N), PLANE_AXES)
    planes, early, late = call(
        ions_kernel,
        (pltpu.VMEM((3, N, N), f32), pltpu.VMEM(EARLY.shape, bf16), pltpu.VMEM(LATE.shape, bf16)),
        smem(5) + vmem(1) + anywhere(5),
        8,
        [pltpu.VMEM((24, N), f32)] * 3 + [pltpu.VMEM((8, N), f32), pltpu.SemaphoreType.DMA((4,))],
    )(
        atom_index,
        direction,
        positions.T,
        z_charge,
        widths,
        profile_table(),
        stay(ion_potential),
        stay(core_density),
        stay(EARLY),
        stay(LATE),
        lines,
    )
    fields, sums = call(
        fields_kernel,
        (shape(SUBS, 2 * N, 2 * N), shape(2 * N, N)),
        smem(1) + vmem(2),
        20,
        [
            pltpu.VMEM((4, 8 * N, N), f32),
            pltpu.VMEM((CELLS, N), f32),
            pltpu.VMEM((24 * PITCH, N), f32),
        ],
    )(dest, arrived, early)
    sums = exchange(sums.reshape(64, 4, N), BAND_AXES + ("xh",)).reshape(2 * N, N)
    sums, spectrum = call(mix_kernel, (shape(64, N), shape(2 * N, N)), vmem(1), 4)(sums)
    spectrum = exchange(spectrum.reshape(8, 32, N), "z").reshape(2 * N, N)
    solved = call(hartree_kernel, shape(3 * N, N), vmem(3), 4)(sums, spectrum, late)
    solved = exchange(solved.reshape(64, 3, 2, N), BAND_AXES + ("xh",)).reshape(3 * N, N)
    outgoing = call(products_kernel, shape(4 * N, N), vmem(5), 20, [pltpu.VMEM((16 * PAIRS, N), f32)])(
        columns, fields, solved, planes, late
    )
    arrived = exchange(outgoing.reshape(N, 4, N), PLANE_AXES).reshape(4 * N, N)
    return call(result_kernel, shape(1, 2, N, 256), vmem(4), 8)(arrived, orbital_tangent, columns, z_forward_table())


def solution(mesh):
    fine = Mesh(mesh.devices.reshape(2, 4, 2, 2, 2, 8), BAND_AXES + GA_AXES)
    lines = P(BAND_AXES, None, None, GA_AXES)
    planes = P(GA_AXES, None, None)
    return jax.shard_map(
        body,
        mesh=fine,
        in_specs=(lines, lines, P(), planes, planes, P(), P(), P(), P(), P()),
        out_specs=lines,
        check_vma=False,
    )
```

```python
import functools
import math

import jax
import jax.numpy as jnp
import ml_dtypes
import numpy as np
from jax import lax
from jax.experimental import pallas as pl
from jax.experimental.pallas import tpu as pltpu
from jax.sharding import Mesh, PartitionSpec as P

N = 128
BANDS = 32
STICKS = 4096
DISP = 8
CUT = N // 4
LINE = 72
SLABS = 68
CELLS = SLABS * LINE
PAIRS = 40
TURNED_ROW = PAIRS + CUT
DUMP = 65 * LINE
CELL = 40.0
SLATER = (3.0 / math.pi) ** (1.0 / 3.0)
FACTOR = (2.0 * math.pi / CELL) ** 2
WEIGHT = 4.0 / N**1.5

BAND_AXES = ("xl", "yh", "yl", "core")
GA_AXES = ("xh", "z")
PLANE_AXES = ("xl", "yl", "core", "xh", "z")
SUBS = 8
PITCH = 136
GROUPS = 16

f32 = jnp.float32
bf16 = jnp.bfloat16


def split_table(table):
    table = np.asarray(table, np.float64)
    high = table.astype(np.float32).astype(ml_dtypes.bfloat16)
    low = (table - high.astype(np.float64)).astype(np.float32).astype(ml_dtypes.bfloat16)
    return np.stack([high, low])


def signed(values):
    return np.where(values >= N // 2, values - N, values)


def angles(rows, columns):
    return 2.0 * np.pi * (np.outer(rows, columns) % N) / N


def plane_of_holder():
    holder = np.arange(N)
    return (holder % GROUPS) * SUBS + holder // GROUPS


def z_inverse_table():
    kept = np.concatenate([np.arange(0, 40), np.arange(96, 128)])
    angle = angles(plane_of_holder(), kept)
    inside = np.abs(signed(kept)) <= CUT
    cosine, sine = np.cos(angle) * inside, np.sin(angle) * inside
    return split_table(np.block([[cosine, -sine], [sine, cosine]]))


def z_forward_table():
    kept = np.concatenate([np.arange(0, 40), np.arange(96, 128)])
    angle = angles(kept, plane_of_holder())
    scale = 1.0 / (WEIGHT * N**3)
    cosine, sine = np.cos(angle) * scale, np.sin(angle) * scale
    return split_table(np.block([[cosine, sine], [-sine, cosine]]))


def box_frequencies(count):
    slot = np.arange(count)
    return slot - CUT, (slot <= 2 * CUT).astype(np.float64)


def y_inverse_table():
    frequency, kept = box_frequencies(LINE)
    angle = angles(frequency, np.arange(N))
    return (np.concatenate([np.cos(angle), np.sin(angle)], 1) * kept[:, None])


def x_inverse_table():
    across = (4 * np.arange(24)[None, :] + np.arange(4)[:, None]).reshape(-1)
    kept = (across <= 2 * CUT).astype(np.float64)
    angle = angles(np.arange(N), across - CUT)
    cosine, sine = WEIGHT * np.cos(angle) * kept, WEIGHT * np.sin(angle) * kept
    return (np.block([[cosine, -sine], [sine, cosine]]))


def x_forward_table():
    slot = np.concatenate([2 * np.arange(40), 2 * np.arange(40) + 1])
    kept = (slot <= 2 * CUT).astype(np.float64)
    angle = angles(slot - CUT, np.arange(N))
    cosine, sine = np.cos(angle) * kept[:, None], np.sin(angle) * kept[:, None]
    real, imag = np.concatenate([cosine, sine], 1), np.concatenate([-sine, cosine], 1)
    real[TURNED_ROW, :N] = 1.0
    imag[TURNED_ROW, N:] = -1.0
    return np.concatenate([real, imag])


def y_forward_table():
    lane = np.arange(N) % 64
    angle = angles(np.arange(N), np.where(lane <= CUT, lane, lane - 64))
    return np.concatenate([np.cos(angle), np.sin(angle)], 1)


def replicate_table():
    table = np.zeros((N, 4, 4, 2, 16))
    for group in range(4):
        for part in range(2):
            for entry in range(16):
                table[group * 32 + entry * 2 + part, group, :, part, entry] = 1.0
    table = table.reshape(N, 2, 2 * N).transpose(1, 0, 2)
    return np.concatenate([table, table], 1).reshape(4 * N, 2 * N)


def real_table():
    row = np.arange(N)
    frequency = np.where(row <= N // 2, row, row - N // 2)
    angle = angles(frequency, np.arange(N))
    values = np.where((row <= N // 2)[:, None], np.cos(angle), np.sin(angle))
    scale = np.where((row == 0) | (row == N // 2), math.sqrt(1.0 / N), math.sqrt(2.0 / N))
    return values * scale[:, None]


def profile_table():
    frequency = np.arange(N) - N // 2
    angle = angles(frequency, np.arange(N))
    return split_table(np.concatenate([np.cos(angle), np.sin(angle)]))


def packed_tables(named, exact={}):
    blocks, places, row = [], {}, 0
    for name, table in named.items():
        parts = split_table(table)
        rows, columns = parts.shape[1:]
        tall = -(-rows // 16) * 16
        block = np.zeros((2, tall, 256), ml_dtypes.bfloat16)
        block[:, :rows, :columns] = parts
        blocks.append(block.reshape(2 * tall, 256))
        places[name] = (row, row + tall, rows, columns)
        row += 2 * tall
    for name, table in exact.items():
        blocks.append(table.astype(ml_dtypes.bfloat16))
        places[name] = row
        row += table.shape[0]
    return np.concatenate(blocks), places


def holder_planes():
    holder = np.arange(N)
    return ((holder % 2) * 8 + holder // 16) * SUBS + (holder // 2) % 8


def early_tables():
    return packed_tables(
        {
            "y_inverse": y_inverse_table(),
            "x_inverse": x_inverse_table(),
            "real": real_table(),
            "real_turned": real_table().T,
        },
        {"replicate": replicate_table()},
    )


def late_tables():
    return packed_tables(
        {
            "real_planes": real_table()[:, holder_planes()],
            "planes_real": real_table().T[holder_planes()],
            "real": real_table(),
            "real_turned": real_table().T,
            "x_forward": x_forward_table(),
            "y_forward": y_forward_table(),
        }

    )


EARLY, EARLY_PLACES = early_tables()
LATE, LATE_PLACES = late_tables()


def table_of(ref, places, name):
    high, low, rows, columns = places[name]
    tall = low - high
    return ref[high : high + tall, 0:columns][0:rows], ref[low : low + tall, 0:columns][0:rows]


def early_table(ref, name):
    return table_of(ref, EARLY_PLACES, name)


def late_table(ref, name):
    return table_of(ref, LATE_PLACES, name)


def halves(values):
    high = values.astype(bf16)
    return high, (values - high.astype(f32)).astype(bf16)


def dot(a, b, dims=((1,), (0,))):
    return lax.dot_general(a, b, (dims, ((), ())), preferred_element_type=f32)


def dot3(left, right, dims=((1,), (0,))):
    return dot(left[0], right[0], dims) + (dot(left[0], right[1], dims) + dot(left[1], right[0], dims))


def pair(ref):
    return ref[0], ref[1]


def stick_frequencies(columns):
    across = columns >> 7
    inplane = columns & (N - 1)
    across = jnp.where(across >= N // 2, across - N, across)
    inplane = jnp.where(inplane >= N // 2, inplane - N, inplane)
    return across, inplane


def kept_rows(shape):
    row = lax.broadcasted_iota(jnp.int32, shape, 0)
    return jnp.where(row >= 40, row + 56 - N, row)


def sphere_radius(columns):
    across, inplane = stick_frequencies(columns)
    frequency = kept_rows((LINE, columns.shape[1]))
    return frequency * frequency + (across * across + inplane * inplane)


def own_columns(columns_ref):
    group = lax.axis_index(GA_AXES)
    return jnp.concatenate([columns_ref[pl.ds(2 * group + half, 1), :] for half in range(2)], 1)


def lines_kernel(orbital_ref, tangent_ref, columns_ref, table_ref, out_ref):
    inside = sphere_radius(own_columns(columns_ref)) <= CUT * CUT
    for which, ref in enumerate((orbital_ref, tangent_ref)):
        parts = []
        for part in range(2):
            kept = jnp.concatenate([ref[0, part, 0:40, :], ref[0, part, 96:128, :]], 0)
            parts.append(jnp.where(inside, kept, 0.0))
        lines = dot3(pair(table_ref), halves(jnp.concatenate(parts, 0)))
        for part in range(2):
            for half in range(2):
                row = half * 4 + which * 2 + part
                out_ref[pl.ds(row, N, stride=8), :] = lines[part * N : (part + 1) * N, half * N : (half + 1) * N]


def circle_reach(slot):
    across = slot - CUT
    return math.isqrt(CUT * CUT - across * across) if abs(across) <= CUT else -1


def fields_kernel(
    dest_ref, lines_ref, tables, fields_ref, sums_ref, turned, grid, middle
):
    replicate = tables[EARLY_PLACES["replicate"] : EARLY_PLACES["replicate"] + 4 * N, :]
    lower = lax.broadcasted_iota(jnp.int32, (8, N), 0) < 4
    for quad in range(4):
        for half in range(2):
            tiles = []
            for group in range(4 * quad, 4 * quad + 4):
                for sub in range(0, SUBS, 2):
                    first, second = lines_ref[sub * GROUPS + group], lines_ref[(sub + 1) * GROUPS + group]
                    if half == 0:
                        tiles.append(jnp.where(lower, first, pltpu.roll(second, 4, 0)))
                    else:
                        tiles.append(jnp.where(lower, pltpu.roll(first, 4, 0), second))
            both = jnp.concatenate(halves(jnp.concatenate(tiles, 0).T), 1)
            base = (quad * 2 + half) * N
            for couple in range(2):
                copies = dot(both, replicate[couple * 2 * N : (couple + 1) * 2 * N])
                for side in range(2):
                    turned[2 * couple + side, base : base + N, :] = copies[:, side * N : (side + 1) * N]
    for quad in range(4):

        def scatter(step, carry, quad=quad):
            for inner in range(8):
                stick = step * 8 + inner
                for slot in range(4):
                    places = dest_ref[(4 * quad + slot) * N + stick]
                    grid[pl.ds(places & 0xFFFF, 1), :] = turned[slot, pl.ds(quad * 2 * N + stick, 1), :]
                    grid[pl.ds(places >> 16, 1), :] = turned[slot, pl.ds((quad * 2 + 1) * N + stick, 1), :]
            return carry

        lax.fori_loop(0, N // 8, scatter, 0)
    lane = lax.broadcasted_iota(jnp.int32, (LINE, N), 1)
    distance = jnp.abs(lax.broadcasted_iota(jnp.int32, (LINE, N), 0) - CUT)
    masks = [lane // 32 == slot for slot in range(4)]
    for step in range(17, 24):
        middle[step * PITCH : step * PITCH + N, :] = jnp.zeros((N, N), f32)
    ytable = early_table(tables, "y_inverse")
    for step in range(17):
        packed = None
        for slot in range(4):
            slab = grid[(4 * step + slot) * LINE : (4 * step + slot + 1) * LINE, :]
            packed = slab if packed is None else jnp.where(masks[slot], slab, packed)
        reach = jnp.full((1, N), circle_reach(4 * step), jnp.int32)
        for slot in range(1, 4):
            reach = jnp.where(masks[slot][0:1], circle_reach(4 * step + slot), reach)
        packed = jnp.where(distance <= reach, packed, 0.0)
        lines = dot3(halves(packed.T), ytable)
        for slot in range(4):
            real, imag = lines[slot * 32 : slot * 32 + 16], lines[slot * 32 + 16 : slot * 32 + 32]
            base = step * PITCH + slot * 16
            middle[base : base + 16, :] = real[:, 0:N] - imag[:, N : 2 * N]
            middle[base + 64 : base + 80, :] = real[:, N : 2 * N] + imag[:, 0:N]
    density = jnp.zeros((N, N), f32)
    response = jnp.zeros((N, N), f32)
    xtable = early_table(tables, "x_inverse")
    for band in range(SUBS):
        sides = []
        for which in range(2):
            rows = []
            for part in range(2):
                for slot in range(4):
                    rows.append(middle[pl.ds(part * 64 + slot * 16 + band * 2 + which, 24, stride=PITCH), :])
            sides.append(jnp.concatenate(rows, 0))
        field = dot3(xtable, halves(jnp.concatenate(sides, 1)))
        fields_ref[band] = field
        first, second = field[:, 0:N], field[:, N : 2 * N]
        density = density + first[0:N] * first[0:N] + first[N : 2 * N] * first[N : 2 * N]
        response = response + first[0:N] * second[0:N] + first[N : 2 * N] * second[N : 2 * N]
    density = density * (1.0 / BANDS)
    response = response * (2.0 / BANDS)
    spectrum = dot3(
        halves(dot3(early_table(tables, "real"), halves(response))), early_table(tables, "real_turned")
    )
    for half in range(2):
        sums_ref[pl.ds(half, 64, stride=4), :] = density[half * 64 : half * 64 + 64]
        sums_ref[pl.ds(2 + half, 64, stride=4), :] = spectrum[half * 64 : half * 64 + 64]


def mix_kernel(arrived_ref, sums_ref, spread_ref):
    for x_low in range(2):
        base = x_low * 128
        rows = [arrived_ref[base + copy * 32 : base + copy * 32 + 32, :] for copy in range(4)]
        sums_ref[x_low * 32 : x_low * 32 + 32, :] = (rows[0] + rows[1]) + (rows[2] + rows[3])
    spectrum = [sums_ref[pl.ds(2 + half, 16, stride=4), :] for half in range(2)]
    for copy in range(8):
        for half in range(2):
            base = copy * 32 + half * 16
            spread_ref[base : base + 16, :] = spectrum[half]


def hartree_kernel(sums_ref, columns_ref, tables_ref, out_ref):
    sides = []
    for half in range(2):
        sides.append(jnp.concatenate([columns_ref[z * 32 + half * 16 : z * 32 + half * 16 + 16, :] for z in range(8)], 0))
    lines = dot3(late_table(tables_ref, "real_planes"), halves(jnp.concatenate(sides, 1)))
    shape = (N, 2 * N)
    row = lax.broadcasted_iota(jnp.int32, shape, 0)
    lane = lax.broadcasted_iota(jnp.int32, shape, 1)
    across = lax.axis_index(BAND_AXES) * 2 + lax.axis_index("xh") + jnp.where(lane >= N, 64, 0)
    inplane = lane & (N - 1)

    def frequency(index):
        return jnp.where(index <= N // 2, index, index - N // 2)

    across, inplane, row = frequency(across), frequency(inplane), frequency(row)
    squares = (row * row + across * across + inplane * inplane).astype(f32)
    kernel = jnp.where(squares == 0.0, 0.0, (4.0 * math.pi / FACTOR) / jnp.where(squares == 0.0, 1.0, squares))
    back = dot3(late_table(tables_ref, "planes_real"), halves(lines * kernel))
    own = lax.axis_index("z")
    mine = back[0:16]
    for z in range(1, 8):
        mine = jnp.where(own == z, back[z * 16 : z * 16 + 16], mine)
    back = mine
    for half in range(2):
        fields = [
            back[:, half * N : (half + 1) * N],
            sums_ref[pl.ds(half, 16, stride=4), :],
            sums_ref[pl.ds(2 + half, 16, stride=4), :],
        ]
        for which, field in enumerate(fields):
            for x_low in range(2):
                for copy in range(4):
                    base = (x_low * 32 + copy * 8) * 6 + which * 2 + half
                    out_ref[pl.ds(base, 8, stride=6), :] = field[x_low * 8 : x_low * 8 + 8]


def own_plane():
    return lax.axis_index(GA_AXES) * SUBS + lax.axis_index(("xl", "yl", "core"))


def ions_kernel(
    atom_ref,
    direction_ref,
    positions_ref,
    charge_ref,
    widths_ref,
    table_ref,
    potential_ref,
    core_ref,
    early_ref,
    late_ref,
    lines_ref,
    out_ref,
    early_out,
    late_out,
    centres,
    spreads,
    marks,
    charges,
    arrivals,
):
    del lines_ref
    own = lax.axis_index(("xl", "yl", "core"))
    copies = [
        pltpu.make_async_copy(potential_ref.at[own], out_ref.at[0], arrivals.at[0]),
        pltpu.make_async_copy(core_ref.at[own], out_ref.at[1], arrivals.at[1]),
        pltpu.make_async_copy(early_ref, early_out, arrivals.at[2]),
        pltpu.make_async_copy(late_ref, late_out, arrivals.at[3]),
    ]
    for copy in copies:
        copy.start()
    for slot in range(DISP):
        atom = atom_ref[slot]
        charges[slot : slot + 1, :] = jnp.full((1, N), charge_ref[atom] * (-1.0 / CELL), f32)
        for axis in range(3):
            row = axis * DISP + slot
            centres[row : row + 1, :] = jnp.full((1, N), positions_ref[axis, atom], f32)
            spreads[row : row + 1, :] = jnp.full((1, N), widths_ref[atom], f32)
            marks[row : row + 1, :] = jnp.full((1, N), jnp.where(direction_ref[slot] == axis, 1.0, 0.0), f32)
    frequency = lax.broadcasted_iota(jnp.int32, (3 * DISP, N), 1) - N // 2
    wavenum = frequency.astype(f32) * (2.0 * math.pi / CELL)
    damping = jnp.exp(-0.5 * (wavenum * spreads[...]) ** 2)
    phase = wavenum * centres[...]
    cosine, sine = damping * jnp.cos(phase), damping * jnp.sin(phase)
    chosen = marks[...] > 0.5
    with_cos = jnp.where(chosen, -wavenum * sine, cosine)
    with_sin = jnp.where(chosen, wavenum * cosine, sine)
    profiles = dot3(halves(jnp.concatenate([with_cos, with_sin], 1)), pair(table_ref))
    along_x, along_y, along_z = profiles[0:8], profiles[8:16], profiles[16:24]
    lane = lax.broadcasted_iota(jnp.int32, (DISP, N), 1)
    here = jnp.sum(jnp.where(lane == own_plane(), along_z, 0.0), 1, keepdims=True)
    scaled = along_y * here * charges[...]
    padding = jnp.zeros((N - DISP, N), f32)
    left = jnp.concatenate([along_x, padding], 0).T
    right = jnp.concatenate([scaled, padding], 0)
    out_ref[2] = dot3(halves(left), halves(right))
    for copy in copies:
        copy.wait()


def products_kernel(columns_ref, fields_ref, solved_ref, planes_ref, tables_ref, out_ref, lines, cells):
    def solved(which):
        return jnp.concatenate([solved_ref[pl.ds(which * 2 + half, 64, stride=6), :] for half in range(2)], 0)

    waves = dot3(late_table(tables_ref, "real_turned"), halves(jnp.concatenate([solved(0), solved(2)], 1)))
    waves = dot3(halves(jnp.concatenate([waves[:, 0:N], waves[:, N : 2 * N]], 0)), late_table(tables_ref, "real"))
    hartree, response = waves[0:N], waves[N : 2 * N]
    total = solved(1) + planes_ref[1]
    root = jnp.exp(jnp.log(total) * (1.0 / 3.0))
    exchange = -SLATER * root
    effective = planes_ref[0] + exchange
    change = exchange / (3.0 * total) * response + hartree + planes_ref[2]
    xtable = late_table(tables_ref, "x_forward")
    ytable = late_table(tables_ref, "y_forward")
    effective2 = jnp.concatenate([effective, effective], 0)
    change2 = jnp.concatenate([change, change], 0)
    lower = lax.broadcasted_iota(jnp.int32, (PAIRS, N), 1) < 64
    for couple in range(SUBS // 2):
        sides = []
        for band in (2 * couple, 2 * couple + 1):
            sides.append(effective2 * fields_ref[band, :, N : 2 * N] + change2 * fields_ref[band, :, 0:N])
        across = dot3(xtable, halves(jnp.concatenate(sides, 1)))
        rows = jnp.concatenate([across[:, 0:N], across[:, N : 2 * N]], 0)
        done = dot3(halves(rows), ytable)
        for side in range(2):
            real = done[side * 4 * PAIRS : side * 4 * PAIRS + 2 * PAIRS]
            imag = done[side * 4 * PAIRS + 2 * PAIRS : (side + 1) * 4 * PAIRS]
            whole = (real[:, 0:N] + imag[:, N : 2 * N], imag[:, 0:N] - real[:, N : 2 * N])
            for part in range(2):
                base = (part * SUBS + 2 * couple + side) * PAIRS
                lines[base : base + PAIRS, :] = jnp.where(lower, whole[part][0:PAIRS], whole[part][PAIRS : 2 * PAIRS])
    for couple in range(CUT + 1):
        for part in range(2):
            at = (couple * 2 + part) * SUBS
            cells[at : at + SUBS, :] = lines[pl.ds(part * SUBS * PAIRS + couple, SUBS, stride=PAIRS), :]
    across, inplane = stick_frequencies(columns_ref[...])
    box = across + CUT
    special = jnp.logical_and(across == 0, inplane == -CUT)
    place = jnp.where(special, 64 + CUT, (box & 1) * 64 + (inplane & 63))
    held = jnp.where(special, CUT, box >> 1)
    held = jnp.where(across * across + inplane * inplane <= CUT * CUT, held, -1)
    sign = jnp.where(special, -1.0, 1.0)
    for vector in range(2 * GROUPS):
        index = jnp.broadcast_to(place[vector : vector + 1], (SUBS, N))
        wanted = jnp.broadcast_to(held[vector : vector + 1], (SUBS, N))
        picked = [jnp.zeros((SUBS, N), f32)] * 2
        for couple in range(CUT + 1):
            mask = wanted == couple
            for part in range(2):
                at = (couple * 2 + part) * SUBS
                found = jnp.take_along_axis(cells[at : at + SUBS, :], index, axis=1)
                picked[part] = jnp.where(mask, found, picked[part])
        picked[1] = picked[1] * sign[vector : vector + 1]
        for part in range(2):
            row = (vector // 2) * 4 + part * 2 + vector % 2
            out_ref[pl.ds(row, SUBS, stride=64), :] = picked[part]


def result_kernel(arrived_ref, tangent_ref, columns_ref, table_ref, out_ref):
    sides = []
    for half in range(2):
        parts = [arrived_ref[pl.ds(part * 2 + half, N, stride=4), :] for part in range(2)]
        sides.append(jnp.concatenate(parts, 0))
    lines = dot3(pair(table_ref), halves(jnp.concatenate(sides, 1)))
    radius = sphere_radius(own_columns(columns_ref))
    inside = radius <= CUT * CUT
    kinetic = (0.5 * FACTOR) * radius.astype(f32)
    for part in range(2):
        kept = jnp.concatenate([tangent_ref[0, part, 0:40, :], tangent_ref[0, part, 96:128, :]], 0)
        rows = jnp.where(inside, lines[part * LINE : (part + 1) * LINE] + kinetic * kept, 0.0)
        out_ref[0, part, 0:40, :] = rows[0:40]
        out_ref[0, part, 40:96, :] = jnp.zeros((56, 256), f32)
        out_ref[0, part, 96:128, :] = rows[40:72]


def vmem(count):
    return [pl.BlockSpec(memory_space=pltpu.VMEM)] * count


def anywhere(count):
    return [pl.BlockSpec(memory_space=pltpu.HBM)] * count


def smem(count):
    return [pl.BlockSpec(memory_space=pltpu.SMEM)] * count


def shape(*dims):
    return jax.ShapeDtypeStruct(dims, f32)


def call(kernel, out_shape, in_specs, mebibytes, scratch=()):
    several = isinstance(out_shape, tuple)
    return pl.pallas_call(
        kernel,
        out_shape=out_shape,
        in_specs=in_specs,
        out_specs=tuple(vmem(len(out_shape))) if several else vmem(1)[0],
        scratch_shapes=scratch,
        compiler_params=pltpu.CompilerParams(vmem_limit_bytes=(mebibytes << 20) or None),
        name=kernel.__name__.removesuffix("_kernel"),
    )


def stay(values):
    return pltpu.with_memory_space_constraint(jnp.asarray(values), pltpu.HBM)


def exchange(values, axes):
    return lax.all_to_all(values, axes, 0, 0, tiled=True)


def body(
    orbitals,
    orbital_tangent,
    stick_columns,
    ion_potential,
    core_density,
    positions,
    z_charge,
    widths,
    atom_index,
    direction,
):
    columns = stick_columns.reshape(STICKS // N, N)
    across, inplane = stick_frequencies(stick_columns)
    cell = (across + CUT) * LINE + (inplane + CUT)
    dest = jnp.where(across * across + inplane * inplane <= CUT * CUT, cell, DUMP).reshape(GROUPS, 2, N)
    dest = (dest[:, 0] + dest[:, 1] * 65536).reshape(-1)
    lines = call(lines_kernel, pltpu.VMEM((N * 8, N), f32), vmem(4), 8)(
        stay(orbitals), stay(orbital_tangent), stay(columns), stay(z_inverse_table())
    )
    arrived = exchange(lines.reshape(N, 8, N), PLANE_AXES)
    planes, early, late = call(
        ions_kernel,
        (pltpu.VMEM((3, N, N), f32), pltpu.VMEM(EARLY.shape, bf16), pltpu.VMEM(LATE.shape, bf16)),
        smem(5) + vmem(1) + anywhere(5),
        8,
        [pltpu.VMEM((24, N), f32)] * 3 + [pltpu.VMEM((8, N), f32), pltpu.SemaphoreType.DMA((4,))],
    )(
        atom_index,
        direction,
        positions.T,
        z_charge,
        widths,
        profile_table(),
        stay(ion_potential),
        stay(core_density),
        stay(EARLY),
        stay(LATE),
        lines,
    )
    fields, sums = call(
        fields_kernel,
        (shape(SUBS, 2 * N, 2 * N), shape(2 * N, N)),
        smem(1) + vmem(2),
        20,
        [
            pltpu.VMEM((4, 8 * N, N), f32),
            pltpu.VMEM((CELLS, N), f32),
            pltpu.VMEM((24 * PITCH, N), f32),
        ],
    )(dest, arrived, early)
    sums = exchange(sums.reshape(64, 4, N), BAND_AXES + ("xh",)).reshape(2 * N, N)
    sums, spectrum = call(mix_kernel, (shape(64, N), shape(2 * N, N)), vmem(1), 4)(sums)
    spectrum = exchange(spectrum.reshape(8, 32, N), "z").reshape(2 * N, N)
    solved = call(hartree_kernel, shape(3 * N, N), vmem(3), 4)(sums, spectrum, late)
    solved = exchange(solved.reshape(64, 3, 2, N), BAND_AXES + ("xh",)).reshape(3 * N, N)
    outgoing = call(products_kernel, shape(4 * N, N), vmem(5), 20, [pltpu.VMEM((16 * PAIRS, N), f32), pltpu.VMEM((66 * SUBS, N), f32)])(
        columns, fields, solved, planes, late
    )
    arrived = exchange(outgoing.reshape(N, 4, N), PLANE_AXES).reshape(4 * N, N)
    return call(result_kernel, shape(1, 2, N, 256), vmem(4), 8)(arrived, orbital_tangent, columns, z_forward_table())


def solution(mesh):
    fine = Mesh(mesh.devices.reshape(2, 4, 2, 2, 2, 8), BAND_AXES + GA_AXES)
    lines = P(BAND_AXES, None, None, GA_AXES)
    planes = P(GA_AXES, None, None)
    return jax.shard_map(
        body,
        mesh=fine,
        in_specs=(lines, lines, P(), planes, planes, P(), P(), P(), P(), P()),
        out_specs=lines,
        check_vma=False,
    )
```

```python
import functools
import math

import jax
import jax.numpy as jnp
import ml_dtypes
import numpy as np
from jax import lax
from jax.experimental import pallas as pl
from jax.experimental.pallas import tpu as pltpu
from jax.sharding import Mesh, PartitionSpec as P

N = 128
BANDS = 32
STICKS = 4096
DISP = 8
CUT = N // 4
LINE = 72
SLABS = 36
CELLS = SLABS * N
PAIRS = 40
TURNED_ROW = PAIRS + CUT
DUMP = 33 * N
CELL = 40.0
SLATER = (3.0 / math.pi) ** (1.0 / 3.0)
FACTOR = (2.0 * math.pi / CELL) ** 2
WEIGHT = 4.0 / N**1.5

BAND_AXES = ("xl", "yh", "yl", "core")
GA_AXES = ("xh", "z")
PLANE_AXES = ("xl", "yl", "core", "xh", "z")
SUBS = 8
PITCH = 264
GROUPS = 16

f32 = jnp.float32
bf16 = jnp.bfloat16


def split_table(table):
    table = np.asarray(table, np.float64)
    high = table.astype(np.float32).astype(ml_dtypes.bfloat16)
    low = (table - high.astype(np.float64)).astype(np.float32).astype(ml_dtypes.bfloat16)
    return np.stack([high, low])


def signed(values):
    return np.where(values >= N // 2, values - N, values)


def angles(rows, columns):
    return 2.0 * np.pi * (np.outer(rows, columns) % N) / N


def plane_of_holder():
    holder = np.arange(N)
    return (holder % GROUPS) * SUBS + holder // GROUPS


def z_inverse_table():
    kept = np.concatenate([np.arange(0, 40), np.arange(96, 128)])
    angle = angles(plane_of_holder(), kept)
    inside = np.abs(signed(kept)) <= CUT
    cosine, sine = np.cos(angle) * inside, np.sin(angle) * inside
    return split_table(np.block([[cosine, -sine], [sine, cosine]]))


def z_forward_table():
    kept = np.concatenate([np.arange(0, 40), np.arange(96, 128)])
    angle = angles(kept, plane_of_holder())
    scale = 1.0 / (WEIGHT * N**3)
    cosine, sine = np.cos(angle) * scale, np.sin(angle) * scale
    return split_table(np.block([[cosine, sine], [-sine, cosine]]))


def box_frequencies(count):
    slot = np.arange(count)
    return slot - CUT, (slot <= 2 * CUT).astype(np.float64)


def y_inverse_table(parity):
    lane = np.arange(64)
    angle = angles(np.where(lane <= CUT, lane, lane - 64), np.arange(N))
    table = np.zeros((N, 2 * N))
    table[parity * 64 : parity * 64 + 64] = np.concatenate([np.cos(angle), np.sin(angle)], 1)
    return table


def x_inverse_table():
    parity, slot, step = np.meshgrid(np.arange(2), np.arange(4), np.arange(16), indexing="ij")
    across = (2 * (4 * step + slot) + parity).reshape(-1)
    special = across == 65
    kept = (across <= 2 * CUT).astype(np.float64)
    angle = angles(np.arange(N), across - CUT)
    cosine, sine = WEIGHT * np.cos(angle) * kept, WEIGHT * np.sin(angle) * kept
    last = np.where(special, -WEIGHT, cosine)
    cosine = np.where(special, WEIGHT, cosine)
    return np.block([[cosine, -sine], [sine, last]])


def x_forward_table():
    slot = np.concatenate([2 * np.arange(40), 2 * np.arange(40) + 1])
    kept = (slot <= 2 * CUT).astype(np.float64)
    angle = angles(slot - CUT, np.arange(N))
    cosine, sine = np.cos(angle) * kept[:, None], np.sin(angle) * kept[:, None]
    real, imag = np.concatenate([cosine, sine], 1), np.concatenate([-sine, cosine], 1)
    real[TURNED_ROW, :N] = 1.0
    imag[TURNED_ROW, N:] = -1.0
    return np.concatenate([real, imag])


def y_forward_table():
    lane = np.arange(N) % 64
    angle = angles(np.arange(N), np.where(lane <= CUT, lane, lane - 64))
    return np.concatenate([np.cos(angle), np.sin(angle)], 1)


def replicate_table():
    table = np.zeros((N, 4, 4, 2, 16))
    for group in range(4):
        for part in range(2):
            for entry in range(16):
                table[group * 32 + entry // 2 * 4 + part * 2 + entry % 2, group, :, part, entry] = 1.0
    table = table.reshape(N, 2, 2 * N).transpose(1, 0, 2)
    return np.concatenate([table, table], 1).reshape(4 * N, 2 * N)


def real_table():
    row = np.arange(N)
    frequency = np.where(row <= N // 2, row, row - N // 2)
    angle = angles(frequency, np.arange(N))
    values = np.where((row <= N // 2)[:, None], np.cos(angle), np.sin(angle))
    scale = np.where((row == 0) | (row == N // 2), math.sqrt(1.0 / N), math.sqrt(2.0 / N))
    return values * scale[:, None]


def profile_table():
    frequency = np.arange(N) - N // 2
    angle = angles(frequency, np.arange(N))
    return split_table(np.concatenate([np.cos(angle), np.sin(angle)]))


def packed_tables(named, exact={}):
    blocks, places, row = [], {}, 0
    for name, table in named.items():
        parts = split_table(table)
        rows, columns = parts.shape[1:]
        tall = -(-rows // 16) * 16
        block = np.zeros((2, tall, 256), ml_dtypes.bfloat16)
        block[:, :rows, :columns] = parts
        blocks.append(block.reshape(2 * tall, 256))
        places[name] = (row, row + tall, rows, columns)
        row += 2 * tall
    for name, table in exact.items():
        blocks.append(table.astype(ml_dtypes.bfloat16))
        places[name] = row
        row += table.shape[0]
    return np.concatenate(blocks), places


def holder_planes():
    holder = np.arange(N)
    return ((holder % 2) * 8 + holder // 16) * SUBS + (holder // 2) % 8


def early_tables():
    return packed_tables(
        {
            "y_even": y_inverse_table(0),
            "y_odd": y_inverse_table(1),
            "x_inverse": x_inverse_table(),
            "real": real_table(),
            "real_turned": real_table().T,
        },
        {"replicate": replicate_table()},
    )


def late_tables():
    return packed_tables(
        {
            "real_planes": real_table()[:, holder_planes()],
            "planes_real": real_table().T[holder_planes()],
            "real": real_table(),
            "real_turned": real_table().T,
            "x_forward": x_forward_table(),
            "y_forward": y_forward_table(),
        }

    )


EARLY, EARLY_PLACES = early_tables()
LATE, LATE_PLACES = late_tables()


def table_of(ref, places, name):
    high, low, rows, columns = places[name]
    tall = low - high
    return ref[high : high + tall, 0:columns][0:rows], ref[low : low + tall, 0:columns][0:rows]


def early_table(ref, name):
    return table_of(ref, EARLY_PLACES, name)


def late_table(ref, name):
    return table_of(ref, LATE_PLACES, name)


def halves(values):
    high = values.astype(bf16)
    return high, (values - high.astype(f32)).astype(bf16)


def dot(a, b, dims=((1,), (0,))):
    return lax.dot_general(a, b, (dims, ((), ())), preferred_element_type=f32)


def dot3(left, right, dims=((1,), (0,))):
    return dot(left[0], right[0], dims) + (dot(left[0], right[1], dims) + dot(left[1], right[0], dims))


def pair(ref):
    return ref[0], ref[1]


def stick_frequencies(columns):
    across = columns >> 7
    inplane = columns & (N - 1)
    across = jnp.where(across >= N // 2, across - N, across)
    inplane = jnp.where(inplane >= N // 2, inplane - N, inplane)
    return across, inplane


def box_cell(across, inplane):
    box = across + CUT
    special = jnp.logical_and(across == 0, inplane == -CUT)
    place = jnp.where(special, 64 + CUT, (box & 1) * 64 + (inplane & 63))
    held = jnp.where(special, CUT, box >> 1)
    held = jnp.where(across * across + inplane * inplane <= CUT * CUT, held, -1)
    return place, held, jnp.where(special, -1.0, 1.0)


def kept_rows(shape):
    row = lax.broadcasted_iota(jnp.int32, shape, 0)
    return jnp.where(row >= 40, row + 56 - N, row)


def sphere_radius(columns):
    across, inplane = stick_frequencies(columns)
    frequency = kept_rows((LINE, columns.shape[1]))
    return frequency * frequency + (across * across + inplane * inplane)


def own_columns(columns_ref):
    group = lax.axis_index(GA_AXES)
    return jnp.concatenate([columns_ref[pl.ds(2 * group + half, 1), :] for half in range(2)], 1)


def lines_kernel(orbital_ref, tangent_ref, columns_ref, table_ref, out_ref):
    own = own_columns(columns_ref)
    inside = sphere_radius(own) <= CUT * CUT
    sign = box_cell(*stick_frequencies(own))[2]
    for which, ref in enumerate((orbital_ref, tangent_ref)):
        parts = []
        for part in range(2):
            kept = jnp.concatenate([ref[0, part, 0:40, :], ref[0, part, 96:128, :]], 0)
            parts.append(jnp.where(inside, kept, 0.0))
        lines = dot3(pair(table_ref), halves(jnp.concatenate(parts, 0)))
        for part in range(2):
            rows = lines[part * N : (part + 1) * N]
            rows = rows if part == 0 else rows * sign
            for half in range(2):
                out_ref[pl.ds(half * 4 + part * 2 + which, N, stride=8), :] = rows[:, half * N : (half + 1) * N]


def fields_kernel(
    dest_ref, lines_ref, tables, sources_ref, fields_ref, sums_ref, turned, grid, found_ref, middle
):
    replicate = tables[EARLY_PLACES["replicate"] : EARLY_PLACES["replicate"] + 4 * N, :]
    row = lax.broadcasted_iota(jnp.int32, (8, N), 0)
    lower = row < 4
    for quad in range(2):
        for half in range(2):
            tiles = []
            for group in range(4 * quad, 4 * quad + 4):
                for sub in range(0, SUBS, 2):
                    first, second = lines_ref[sub * GROUPS + group], lines_ref[(sub + 1) * GROUPS + group]
                    if half == 0:
                        tiles.append(jnp.where(lower, first, pltpu.roll(second, 4, 0)))
                    else:
                        tiles.append(jnp.where(lower, pltpu.roll(first, 4, 0), second))
            both = jnp.concatenate(halves(jnp.concatenate(tiles, 0).T), 1)
            base = (quad * 2 + half) * N
            for couple in range(2):
                copies = dot(both, replicate[couple * 2 * N : (couple + 1) * 2 * N])
                for side in range(2):
                    turned[2 * couple + side, base : base + N, :] = copies[:, side * N : (side + 1) * N]
    grid[...] = jnp.zeros_like(grid)
    found_ref[33 * 32 :, :] = jnp.zeros((3 * 32, N), f32)

    def scatter(word):
        quad, stick, slot = word // (4 * N), word // 4 % N, word % 4
        places = dest_ref[(4 * quad + slot) * N + stick]
        grid[pl.ds(places & 0xFFFF, 1), :] = turned[slot, pl.ds(quad * 2 * N + stick, 1), :]
        grid[pl.ds(places >> 16, 1), :] = turned[slot, pl.ds((quad * 2 + 1) * N + stick, 1), :]

    upper = jnp.where(lower, 0, -1)
    word = 0
    for couple in range(CUT + 1):
        vectors = jnp.broadcast_to(sources_ref[0, couple : couple + 1, :], (8, N)) + upper
        index = jnp.broadcast_to(sources_ref[1, couple : couple + 1, :], (8, N))
        picked = [jnp.zeros((8, N), f32)] * SUBS
        for group in range(8):
            mask = vectors == 2 * group + 1
            for sub in range(SUBS):
                cells = jnp.take_along_axis(lines_ref[sub * GROUPS + 8 + group], index, axis=1)
                picked[sub] = jnp.where(mask, cells, picked[sub])
                if sub % 2 == 1 and word < 8 * N:
                    scatter(word)
                    word += 1
        picked = [part + pltpu.roll(part, 4, 0) for part in picked]
        for four in range(2):
            a, b, c, d = picked[4 * four : 4 * four + 4]
            real = jnp.where(row < 2, a, jnp.where(lower, pltpu.roll(b, 2, 0), jnp.where(row < 6, c, pltpu.roll(d, 2, 0))))
            imag = jnp.where(row < 2, pltpu.roll(a, 6, 0), jnp.where(lower, b, jnp.where(row < 6, pltpu.roll(c, 6, 0), d)))
            base = couple * 32 + four * 8
            found_ref[base : base + 8, :] = real
            found_ref[base + 16 : base + 24, :] = imag
    lane = lax.broadcasted_iota(jnp.int32, (N, N), 1)
    masks = [lane // 32 == slot for slot in range(4)]
    for step in range(9, 16):
        middle[step * PITCH : step * PITCH + 2 * N, :] = jnp.zeros((2 * N, N), f32)
    ytables = [early_table(tables, "y_even"), early_table(tables, "y_odd")]
    for step in range(9):
        packed = None
        for slot in range(4):
            slab = grid[(4 * step + slot) * N : (4 * step + slot + 1) * N, :]
            packed = slab if packed is None else jnp.where(masks[slot], slab, packed)
        lines = halves(packed.T + found_ref[step * N : (step + 1) * N, :])
        for parity in range(2):
            done = dot3(lines, ytables[parity])
            for slot in range(4):
                real, imag = done[slot * 32 : slot * 32 + 16], done[slot * 32 + 16 : slot * 32 + 32]
                base = step * PITCH + parity * N + slot * 16
                middle[base : base + 16, :] = real[:, 0:N] - imag[:, N : 2 * N]
                middle[base + 64 : base + 80, :] = real[:, N : 2 * N] + imag[:, 0:N]
    density = jnp.zeros((N, N), f32)
    response = jnp.zeros((N, N), f32)
    xtable = early_table(tables, "x_inverse")
    for band in range(SUBS):
        sides = []
        for which in range(2):
            rows = []
            for part in range(2):
                for parity in range(2):
                    for slot in range(4):
                        base = parity * N + part * 64 + slot * 16 + band * 2 + which
                        rows.append(middle[pl.ds(base, 16, stride=PITCH), :])
            sides.append(jnp.concatenate(rows, 0))
        field = dot3(xtable, halves(jnp.concatenate(sides, 1)))
        fields_ref[band] = field
        first, second = field[:, 0:N], field[:, N : 2 * N]
        density = density + first[0:N] * first[0:N] + first[N : 2 * N] * first[N : 2 * N]
        response = response + first[0:N] * second[0:N] + first[N : 2 * N] * second[N : 2 * N]
    density = density * (1.0 / BANDS)
    response = response * (2.0 / BANDS)
    spectrum = dot3(
        halves(dot3(early_table(tables, "real"), halves(response))), early_table(tables, "real_turned")
    )
    for half in range(2):
        sums_ref[pl.ds(half, 64, stride=4), :] = density[half * 64 : half * 64 + 64]
        sums_ref[pl.ds(2 + half, 64, stride=4), :] = spectrum[half * 64 : half * 64 + 64]


def mix_kernel(arrived_ref, sums_ref, spread_ref):
    for x_low in range(2):
        base = x_low * 128
        rows = [arrived_ref[base + copy * 32 : base + copy * 32 + 32, :] for copy in range(4)]
        sums_ref[x_low * 32 : x_low * 32 + 32, :] = (rows[0] + rows[1]) + (rows[2] + rows[3])
    spectrum = [sums_ref[pl.ds(2 + half, 16, stride=4), :] for half in range(2)]
    for copy in range(8):
        for half in range(2):
            base = copy * 32 + half * 16
            spread_ref[base : base + 16, :] = spectrum[half]


def hartree_kernel(sums_ref, columns_ref, tables_ref, out_ref):
    sides = []
    for half in range(2):
        sides.append(jnp.concatenate([columns_ref[z * 32 + half * 16 : z * 32 + half * 16 + 16, :] for z in range(8)], 0))
    lines = dot3(late_table(tables_ref, "real_planes"), halves(jnp.concatenate(sides, 1)))
    shape = (N, 2 * N)
    row = lax.broadcasted_iota(jnp.int32, shape, 0)
    lane = lax.broadcasted_iota(jnp.int32, shape, 1)
    across = lax.axis_index(BAND_AXES) * 2 + lax.axis_index("xh") + jnp.where(lane >= N, 64, 0)
    inplane = lane & (N - 1)

    def frequency(index):
        return jnp.where(index <= N // 2, index, index - N // 2)

    across, inplane, row = frequency(across), frequency(inplane), frequency(row)
    squares = (row * row + across * across + inplane * inplane).astype(f32)
    kernel = jnp.where(squares == 0.0, 0.0, (4.0 * math.pi / FACTOR) / jnp.where(squares == 0.0, 1.0, squares))
    back = dot3(late_table(tables_ref, "planes_real"), halves(lines * kernel))
    own = lax.axis_index("z")
    mine = back[0:16]
    for z in range(1, 8):
        mine = jnp.where(own == z, back[z * 16 : z * 16 + 16], mine)
    back = mine
    for half in range(2):
        fields = [
            back[:, half * N : (half + 1) * N],
            sums_ref[pl.ds(half, 16, stride=4), :],
            sums_ref[pl.ds(2 + half, 16, stride=4), :],
        ]
        for which, field in enumerate(fields):
            for x_low in range(2):
                for copy in range(4):
                    base = (x_low * 32 + copy * 8) * 6 + which * 2 + half
                    out_ref[pl.ds(base, 8, stride=6), :] = field[x_low * 8 : x_low * 8 + 8]


def own_plane():
    return lax.axis_index(GA_AXES) * SUBS + lax.axis_index(("xl", "yl", "core"))


def ions_kernel(
    atom_ref,
    direction_ref,
    positions_ref,
    charge_ref,
    widths_ref,
    table_ref,
    potential_ref,
    core_ref,
    early_ref,
    late_ref,
    lines_ref,
    columns_ref,
    out_ref,
    early_out,
    late_out,
    sources_ref,
    centres,
    spreads,
    marks,
    charges,
    arrivals,
):
    del lines_ref
    own = lax.axis_index(("xl", "yl", "core"))
    copies = [
        pltpu.make_async_copy(potential_ref.at[own], out_ref.at[0], arrivals.at[0]),
        pltpu.make_async_copy(core_ref.at[own], out_ref.at[1], arrivals.at[1]),
        pltpu.make_async_copy(early_ref, early_out, arrivals.at[2]),
        pltpu.make_async_copy(late_ref, late_out, arrivals.at[3]),
    ]
    for copy in copies:
        copy.start()
    for slot in range(DISP):
        atom = atom_ref[slot]
        charges[slot : slot + 1, :] = jnp.full((1, N), charge_ref[atom] * (-1.0 / CELL), f32)
        for axis in range(3):
            row = axis * DISP + slot
            centres[row : row + 1, :] = jnp.full((1, N), positions_ref[axis, atom], f32)
            spreads[row : row + 1, :] = jnp.full((1, N), widths_ref[atom], f32)
            marks[row : row + 1, :] = jnp.full((1, N), jnp.where(direction_ref[slot] == axis, 1.0, 0.0), f32)
    frequency = lax.broadcasted_iota(jnp.int32, (3 * DISP, N), 1) - N // 2
    wavenum = frequency.astype(f32) * (2.0 * math.pi / CELL)
    damping = jnp.exp(-0.5 * (wavenum * spreads[...]) ** 2)
    phase = wavenum * centres[...]
    cosine, sine = damping * jnp.cos(phase), damping * jnp.sin(phase)
    chosen = marks[...] > 0.5
    with_cos = jnp.where(chosen, -wavenum * sine, cosine)
    with_sin = jnp.where(chosen, wavenum * cosine, sine)
    profiles = dot3(halves(jnp.concatenate([with_cos, with_sin], 1)), pair(table_ref))
    along_x, along_y, along_z = profiles[0:8], profiles[8:16], profiles[16:24]
    lane = lax.broadcasted_iota(jnp.int32, (DISP, N), 1)
    here = jnp.sum(jnp.where(lane == own_plane(), along_z, 0.0), 1, keepdims=True)
    scaled = along_y * here * charges[...]
    padding = jnp.zeros((N - DISP, N), f32)
    left = jnp.concatenate([along_x, padding], 0).T
    right = jnp.concatenate([scaled, padding], 0)
    out_ref[2] = dot3(halves(left), halves(right))
    place, held, ignored = box_cell(*stick_frequencies(columns_ref[GROUPS : 2 * GROUPS, :]))
    pairs = lax.broadcasted_iota(jnp.int32, (PAIRS, N), 0)
    lanes = lax.broadcasted_iota(jnp.int32, (PAIRS, N), 1).astype(f32)
    places = lax.broadcasted_iota(jnp.int32, (N, N), 0)
    found = jnp.zeros((2 * PAIRS, N), f32)
    for vector in range(GROUPS):
        here = held[vector : vector + 1] == pairs
        marks = jnp.concatenate([jnp.where(here, vector + 1.0, 0.0), jnp.where(here, lanes, 0.0)], 0).astype(bf16)
        spots = jnp.where(place[vector : vector + 1] == places, 1.0, 0.0).astype(bf16)
        found = found + dot(marks, spots, ((1,), (1,)))
    sources_ref[0] = found[0:PAIRS].astype(jnp.int32)
    sources_ref[1] = found[PAIRS : 2 * PAIRS].astype(jnp.int32)
    for copy in copies:
        copy.wait()


def products_kernel(columns_ref, fields_ref, solved_ref, planes_ref, tables_ref, out_ref, lines, cells):
    def solved(which):
        return jnp.concatenate([solved_ref[pl.ds(which * 2 + half, 64, stride=6), :] for half in range(2)], 0)

    waves = dot3(late_table(tables_ref, "real_turned"), halves(jnp.concatenate([solved(0), solved(2)], 1)))
    waves = dot3(halves(jnp.concatenate([waves[:, 0:N], waves[:, N : 2 * N]], 0)), late_table(tables_ref, "real"))
    hartree, response = waves[0:N], waves[N : 2 * N]
    total = solved(1) + planes_ref[1]
    root = jnp.exp(jnp.log(total) * (1.0 / 3.0))
    exchange = -SLATER * root
    effective = planes_ref[0] + exchange
    change = exchange / (3.0 * total) * response + hartree + planes_ref[2]
    xtable = late_table(tables_ref, "x_forward")
    ytable = late_table(tables_ref, "y_forward")
    effective2 = jnp.concatenate([effective, effective], 0)
    change2 = jnp.concatenate([change, change], 0)
    lower = lax.broadcasted_iota(jnp.int32, (PAIRS, N), 1) < 64
    for couple in range(SUBS // 2):
        sides = []
        for band in (2 * couple, 2 * couple + 1):
            sides.append(effective2 * fields_ref[band, :, N : 2 * N] + change2 * fields_ref[band, :, 0:N])
        across = dot3(xtable, halves(jnp.concatenate(sides, 1)))
        rows = jnp.concatenate([across[:, 0:N], across[:, N : 2 * N]], 0)
        done = dot3(halves(rows), ytable)
        for side in range(2):
            real = done[side * 4 * PAIRS : side * 4 * PAIRS + 2 * PAIRS]
            imag = done[side * 4 * PAIRS + 2 * PAIRS : (side + 1) * 4 * PAIRS]
            whole = (real[:, 0:N] + imag[:, N : 2 * N], imag[:, 0:N] - real[:, N : 2 * N])
            for part in range(2):
                base = (part * SUBS + 2 * couple + side) * PAIRS
                lines[base : base + PAIRS, :] = jnp.where(lower, whole[part][0:PAIRS], whole[part][PAIRS : 2 * PAIRS])
    for couple in range(CUT + 1):
        for part in range(2):
            at = (couple * 2 + part) * SUBS
            cells[at : at + SUBS, :] = lines[pl.ds(part * SUBS * PAIRS + couple, SUBS, stride=PAIRS), :]
    across, inplane = stick_frequencies(columns_ref[...])
    place, held, sign = box_cell(across, inplane)
    for vector in range(2 * GROUPS):
        index = jnp.broadcast_to(place[vector : vector + 1], (SUBS, N))
        wanted = jnp.broadcast_to(held[vector : vector + 1], (SUBS, N))
        picked = [jnp.zeros((SUBS, N), f32)] * 2
        for couple in range(CUT + 1):
            mask = wanted == couple
            for part in range(2):
                at = (couple * 2 + part) * SUBS
                found = jnp.take_along_axis(cells[at : at + SUBS, :], index, axis=1)
                picked[part] = jnp.where(mask, found, picked[part])
        picked[1] = picked[1] * sign[vector : vector + 1]
        for part in range(2):
            row = (vector // 2) * 4 + part * 2 + vector % 2
            out_ref[pl.ds(row, SUBS, stride=64), :] = picked[part]


def result_kernel(arrived_ref, tangent_ref, columns_ref, table_ref, out_ref):
    sides = []
    for half in range(2):
        parts = [arrived_ref[pl.ds(part * 2 + half, N, stride=4), :] for part in range(2)]
        sides.append(jnp.concatenate(parts, 0))
    lines = dot3(pair(table_ref), halves(jnp.concatenate(sides, 1)))
    radius = sphere_radius(own_columns(columns_ref))
    inside = radius <= CUT * CUT
    kinetic = (0.5 * FACTOR) * radius.astype(f32)
    for part in range(2):
        kept = jnp.concatenate([tangent_ref[0, part, 0:40, :], tangent_ref[0, part, 96:128, :]], 0)
        rows = jnp.where(inside, lines[part * LINE : (part + 1) * LINE] + kinetic * kept, 0.0)
        out_ref[0, part, 0:40, :] = rows[0:40]
        out_ref[0, part, 40:96, :] = jnp.zeros((56, 256), f32)
        out_ref[0, part, 96:128, :] = rows[40:72]


def vmem(count):
    return [pl.BlockSpec(memory_space=pltpu.VMEM)] * count


def anywhere(count):
    return [pl.BlockSpec(memory_space=pltpu.HBM)] * count


def smem(count):
    return [pl.BlockSpec(memory_space=pltpu.SMEM)] * count


def shape(*dims):
    return jax.ShapeDtypeStruct(dims, f32)


def call(kernel, out_shape, in_specs, mebibytes, scratch=()):
    several = isinstance(out_shape, tuple)
    return pl.pallas_call(
        kernel,
        out_shape=out_shape,
        in_specs=in_specs,
        out_specs=tuple(vmem(len(out_shape))) if several else vmem(1)[0],
        scratch_shapes=scratch,
        compiler_params=pltpu.CompilerParams(vmem_limit_bytes=(mebibytes << 20) or None),
        name=kernel.__name__.removesuffix("_kernel"),
    )


def stay(values):
    return pltpu.with_memory_space_constraint(jnp.asarray(values), pltpu.HBM)


def exchange(values, axes):
    return lax.all_to_all(values, axes, 0, 0, tiled=True)


def body(
    orbitals,
    orbital_tangent,
    stick_columns,
    ion_potential,
    core_density,
    positions,
    z_charge,
    widths,
    atom_index,
    direction,
):
    columns = stick_columns.reshape(STICKS // N, N)
    across, inplane = stick_frequencies(stick_columns)
    place, held, ignored = box_cell(across, inplane)
    dest = jnp.where(held >= 0, held * N + place, DUMP).reshape(GROUPS, 2, N)[:8]
    dest = (dest[:, 0] + dest[:, 1] * 65536).reshape(-1)
    lines = call(lines_kernel, pltpu.VMEM((N * 8, N), f32), vmem(4), 8)(
        stay(orbitals), stay(orbital_tangent), stay(columns), stay(z_inverse_table())
    )
    arrived = exchange(lines.reshape(N, 8, N), PLANE_AXES)
    planes, early, late, sources = call(
        ions_kernel,
        (pltpu.VMEM((3, N, N), f32), pltpu.VMEM(EARLY.shape, bf16), pltpu.VMEM(LATE.shape, bf16), pltpu.VMEM((2, PAIRS, N), jnp.int32)),
        smem(5) + vmem(1) + anywhere(5) + vmem(1),
        8,
        [pltpu.VMEM((24, N), f32)] * 3 + [pltpu.VMEM((8, N), f32), pltpu.SemaphoreType.DMA((4,))],
    )(
        atom_index,
        direction,
        positions.T,
        z_charge,
        widths,
        profile_table(),
        stay(ion_potential),
        stay(core_density),
        stay(EARLY),
        stay(LATE),
        lines,
        columns,
    )
    fields, sums = call(
        fields_kernel,
        (shape(SUBS, 2 * N, 2 * N), shape(2 * N, N)),
        smem(1) + vmem(3),
        20,
        [
            pltpu.VMEM((4, 4 * N, N), f32),
            pltpu.VMEM((CELLS, N), f32),
            pltpu.VMEM((SLABS * 32, N), f32),
            pltpu.VMEM((16 * PITCH, N), f32),
        ],
    )(dest, arrived, early, sources)
    sums = exchange(sums.reshape(64, 4, N), BAND_AXES + ("xh",)).reshape(2 * N, N)
    sums, spectrum = call(mix_kernel, (shape(64, N), shape(2 * N, N)), vmem(1), 4)(sums)
    spectrum = exchange(spectrum.reshape(8, 32, N), "z").reshape(2 * N, N)
    solved = call(hartree_kernel, shape(3 * N, N), vmem(3), 4)(sums, spectrum, late)
    solved = exchange(solved.reshape(64, 3, 2, N), BAND_AXES + ("xh",)).reshape(3 * N, N)
    outgoing = call(products_kernel, shape(4 * N, N), vmem(5), 20, [pltpu.VMEM((16 * PAIRS, N), f32), pltpu.VMEM((66 * SUBS, N), f32)])(
        columns, fields, solved, planes, late
    )
    arrived = exchange(outgoing.reshape(N, 4, N), PLANE_AXES).reshape(4 * N, N)
    return call(result_kernel, shape(1, 2, N, 256), vmem(4), 8)(arrived, orbital_tangent, columns, z_forward_table())


def solution(mesh):
    fine = Mesh(mesh.devices.reshape(2, 4, 2, 2, 2, 8), BAND_AXES + GA_AXES)
    lines = P(BAND_AXES, None, None, GA_AXES)
    planes = P(GA_AXES, None, None)
    return jax.shard_map(
        body,
        mesh=fine,
        in_specs=(lines, lines, P(), planes, planes, P(), P(), P(), P(), P()),
        out_specs=lines,
        check_vma=False,
    )
```

```python
import functools
import math

import jax
import jax.numpy as jnp
import ml_dtypes
import numpy as np
from jax import lax
from jax.experimental import pallas as pl
from jax.experimental.pallas import tpu as pltpu
from jax.sharding import Mesh, PartitionSpec as P

N = 128
BANDS = 32
STICKS = 4096
DISP = 8
CUT = N // 4
LINE = 72
SLABS = 36
CELLS = SLABS * N
PAIRS = 40
TURNED_ROW = PAIRS + CUT
DUMP = 33 * N
CELL = 40.0
SLATER = (3.0 / math.pi) ** (1.0 / 3.0)
FACTOR = (2.0 * math.pi / CELL) ** 2
WEIGHT = 4.0 / N**1.5

BAND_AXES = ("xl", "yh", "yl", "core")
GA_AXES = ("xh", "z")
PLANE_AXES = ("xl", "yl", "core", "xh", "z")
SUBS = 8
PITCH = 264
GROUPS = 16

f32 = jnp.float32
bf16 = jnp.bfloat16


def split_table(table):
    table = np.asarray(table, np.float64)
    high = table.astype(np.float32).astype(ml_dtypes.bfloat16)
    low = (table - high.astype(np.float64)).astype(np.float32).astype(ml_dtypes.bfloat16)
    return np.stack([high, low])


def signed(values):
    return np.where(values >= N // 2, values - N, values)


def angles(rows, columns):
    return 2.0 * np.pi * (np.outer(rows, columns) % N) / N


def plane_of_holder():
    holder = np.arange(N)
    return (holder % GROUPS) * SUBS + holder // GROUPS


def z_inverse_table():
    kept = np.concatenate([np.arange(0, 40), np.arange(96, 128)])
    angle = angles(plane_of_holder(), kept)
    inside = np.abs(signed(kept)) <= CUT
    cosine, sine = np.cos(angle) * inside, np.sin(angle) * inside
    return split_table(np.block([[cosine, -sine], [sine, cosine]]))


def z_forward_table():
    kept = np.concatenate([np.arange(0, 40), np.arange(96, 128)])
    angle = angles(kept, plane_of_holder())
    scale = 1.0 / (WEIGHT * N**3)
    cosine, sine = np.cos(angle) * scale, np.sin(angle) * scale
    return split_table(np.block([[cosine, sine], [-sine, cosine]]))


def box_frequencies(count):
    slot = np.arange(count)
    return slot - CUT, (slot <= 2 * CUT).astype(np.float64)


def y_inverse_table(parity):
    lane = np.arange(64)
    angle = angles(np.where(lane <= CUT, lane, lane - 64), np.arange(N))
    table = np.zeros((N, 2 * N))
    table[parity * 64 : parity * 64 + 64] = np.concatenate([np.cos(angle), np.sin(angle)], 1)
    return table


def x_inverse_table():
    parity, slot, step = np.meshgrid(np.arange(2), np.arange(4), np.arange(16), indexing="ij")
    across = (2 * (4 * step + slot) + parity).reshape(-1)
    special = across == 65
    kept = (across <= 2 * CUT).astype(np.float64)
    angle = angles(np.arange(N), across - CUT)
    cosine, sine = WEIGHT * np.cos(angle) * kept, WEIGHT * np.sin(angle) * kept
    last = np.where(special, -WEIGHT, cosine)
    cosine = np.where(special, WEIGHT, cosine)
    return np.block([[cosine, -sine], [sine, last]])


def x_forward_table():
    slot = np.concatenate([2 * np.arange(40), 2 * np.arange(40) + 1])
    kept = (slot <= 2 * CUT).astype(np.float64)
    angle = angles(slot - CUT, np.arange(N))
    cosine, sine = np.cos(angle) * kept[:, None], np.sin(angle) * kept[:, None]
    real, imag = np.concatenate([cosine, sine], 1), np.concatenate([-sine, cosine], 1)
    real[TURNED_ROW, :N] = 1.0
    imag[TURNED_ROW, N:] = -1.0
    return np.concatenate([real, imag])


def y_forward_table():
    lane = np.arange(N) % 64
    angle = angles(np.arange(N), np.where(lane <= CUT, lane, lane - 64))
    return np.concatenate([np.cos(angle), np.sin(angle)], 1)


def replicate_table():
    table = np.zeros((N, 4, 4, 2, 16))
    for group in range(4):
        for part in range(2):
            for entry in range(16):
                table[group * 32 + entry // 2 * 4 + part * 2 + entry % 2, group, :, part, entry] = 1.0
    table = table.reshape(N, 2, 2 * N).transpose(1, 0, 2)
    return np.concatenate([table, table], 1).reshape(4 * N, 2 * N)


def real_table():
    row = np.arange(N)
    frequency = np.where(row <= N // 2, row, row - N // 2)
    angle = angles(frequency, np.arange(N))
    values = np.where((row <= N // 2)[:, None], np.cos(angle), np.sin(angle))
    scale = np.where((row == 0) | (row == N // 2), math.sqrt(1.0 / N), math.sqrt(2.0 / N))
    return values * scale[:, None]


def profile_table():
    frequency = np.arange(N) - N // 2
    angle = angles(frequency, np.arange(N))
    return split_table(np.concatenate([np.cos(angle), np.sin(angle)]))


def packed_tables(named, exact={}):
    blocks, places, row = [], {}, 0
    for name, table in named.items():
        parts = split_table(table)
        rows, columns = parts.shape[1:]
        tall = -(-rows // 16) * 16
        block = np.zeros((2, tall, 256), ml_dtypes.bfloat16)
        block[:, :rows, :columns] = parts
        blocks.append(block.reshape(2 * tall, 256))
        places[name] = (row, row + tall, rows, columns)
        row += 2 * tall
    for name, table in exact.items():
        blocks.append(table.astype(ml_dtypes.bfloat16))
        places[name] = row
        row += table.shape[0]
    return np.concatenate(blocks), places


def holder_planes():
    holder = np.arange(N)
    return ((holder % 2) * 8 + holder // 16) * SUBS + (holder // 2) % 8


def early_tables():
    return packed_tables(
        {
            "y_even": y_inverse_table(0),
            "y_odd": y_inverse_table(1),
            "x_inverse": x_inverse_table(),
            "real": real_table(),
            "real_turned": real_table().T,
        },
        {"replicate": replicate_table()},
    )


def late_tables():
    return packed_tables(
        {
            "real_planes": real_table()[:, holder_planes()],
            "planes_real": real_table().T[holder_planes()],
            "real": real_table(),
            "real_turned": real_table().T,
            "x_forward": x_forward_table(),
            "y_forward": y_forward_table(),
        }

    )


EARLY, EARLY_PLACES = early_tables()
LATE, LATE_PLACES = late_tables()


def table_of(ref, places, name):
    high, low, rows, columns = places[name]
    tall = low - high
    return ref[high : high + tall, 0:columns][0:rows], ref[low : low + tall, 0:columns][0:rows]


def early_table(ref, name):
    return table_of(ref, EARLY_PLACES, name)


def late_table(ref, name):
    return table_of(ref, LATE_PLACES, name)


def halves(values):
    high = values.astype(bf16)
    return high, (values - high.astype(f32)).astype(bf16)


def dot(a, b, dims=((1,), (0,))):
    return lax.dot_general(a, b, (dims, ((), ())), preferred_element_type=f32)


def dot3(left, right, dims=((1,), (0,))):
    return dot(left[0], right[0], dims) + (dot(left[0], right[1], dims) + dot(left[1], right[0], dims))


def pair(ref):
    return ref[0], ref[1]


def stick_frequencies(columns):
    across = columns >> 7
    inplane = columns & (N - 1)
    across = jnp.where(across >= N // 2, across - N, across)
    inplane = jnp.where(inplane >= N // 2, inplane - N, inplane)
    return across, inplane


def box_cell(across, inplane):
    box = across + CUT
    special = jnp.logical_and(across == 0, inplane == -CUT)
    place = jnp.where(special, 64 + CUT, (box & 1) * 64 + (inplane & 63))
    held = jnp.where(special, CUT, box >> 1)
    held = jnp.where(across * across + inplane * inplane <= CUT * CUT, held, -1)
    return place, held, jnp.where(special, -1.0, 1.0)


def kept_rows(shape):
    row = lax.broadcasted_iota(jnp.int32, shape, 0)
    return jnp.where(row >= 40, row + 56 - N, row)


def sphere_radius(columns):
    across, inplane = stick_frequencies(columns)
    frequency = kept_rows((LINE, columns.shape[1]))
    return frequency * frequency + (across * across + inplane * inplane)


def own_columns(columns_ref):
    group = lax.axis_index(GA_AXES)
    return jnp.concatenate([columns_ref[pl.ds(2 * group + half, 1), :] for half in range(2)], 1)


def lines_kernel(orbital_ref, tangent_ref, columns_ref, table_ref, out_ref):
    own = own_columns(columns_ref)
    inside = sphere_radius(own) <= CUT * CUT
    sign = box_cell(*stick_frequencies(own))[2]
    for which, ref in enumerate((orbital_ref, tangent_ref)):
        parts = []
        for part in range(2):
            kept = jnp.concatenate([ref[0, part, 0:40, :], ref[0, part, 96:128, :]], 0)
            parts.append(jnp.where(inside, kept, 0.0))
        lines = dot3(pair(table_ref), halves(jnp.concatenate(parts, 0)))
        for part in range(2):
            rows = lines[part * N : (part + 1) * N]
            rows = rows if part == 0 else rows * sign
            for half in range(2):
                out_ref[pl.ds(half * 4 + part * 2 + which, N, stride=8), :] = rows[:, half * N : (half + 1) * N]


def fields_kernel(
    dest_ref, lines_ref, tables, sources_ref, fields_ref, sums_ref, turned, grid, found_ref, middle
):
    replicate = tables[EARLY_PLACES["replicate"] : EARLY_PLACES["replicate"] + 4 * N, :]
    row = lax.broadcasted_iota(jnp.int32, (8, N), 0)
    lower = row < 4
    for quad in range(2):
        for half in range(2):
            tiles = []
            for group in range(4 * quad, 4 * quad + 4):
                for sub in range(0, SUBS, 2):
                    first, second = lines_ref[sub * GROUPS + group], lines_ref[(sub + 1) * GROUPS + group]
                    if half == 0:
                        tiles.append(jnp.where(lower, first, pltpu.roll(second, 4, 0)))
                    else:
                        tiles.append(jnp.where(lower, pltpu.roll(first, 4, 0), second))
            both = jnp.concatenate(halves(jnp.concatenate(tiles, 0).T), 1)
            base = (quad * 2 + half) * N
            for couple in range(2):
                copies = dot(both, replicate[couple * 2 * N : (couple + 1) * 2 * N])
                for side in range(2):
                    turned[2 * couple + side, base : base + N, :] = copies[:, side * N : (side + 1) * N]
    grid[...] = jnp.zeros_like(grid)
    found_ref[33 * 32 :, :] = jnp.zeros((3 * 32, N), f32)

    def scatter(word):
        quad, stick, slot = word // (4 * N), word // 4 % N, word % 4
        places = dest_ref[(4 * quad + slot) * N + stick]
        grid[pl.ds(places & 0xFFFF, 1), :] = turned[slot, pl.ds(quad * 2 * N + stick, 1), :]
        grid[pl.ds(places >> 16, 1), :] = turned[slot, pl.ds((quad * 2 + 1) * N + stick, 1), :]

    upper = jnp.where(lower, 0, -1)
    word = 0
    for couple in range(CUT + 1):
        vectors = jnp.broadcast_to(sources_ref[0, couple : couple + 1, :], (8, N)) + upper
        index = jnp.broadcast_to(sources_ref[1, couple : couple + 1, :], (8, N))
        picked = [jnp.zeros((8, N), f32)] * SUBS
        for group in range(8):
            mask = vectors == 2 * group + 1
            for sub in range(SUBS):
                cells = jnp.take_along_axis(lines_ref[sub * GROUPS + 8 + group], index, axis=1)
                picked[sub] = jnp.where(mask, cells, picked[sub])
                if sub % 2 == 1 and word < 8 * N:
                    scatter(word)
                    word += 1
        picked = [part + pltpu.roll(part, 4, 0) for part in picked]
        for four in range(2):
            a, b, c, d = picked[4 * four : 4 * four + 4]
            real = jnp.where(row < 2, a, jnp.where(lower, pltpu.roll(b, 2, 0), jnp.where(row < 6, c, pltpu.roll(d, 2, 0))))
            imag = jnp.where(row < 2, pltpu.roll(a, 6, 0), jnp.where(lower, b, jnp.where(row < 6, pltpu.roll(c, 6, 0), d)))
            base = couple * 32 + four * 8
            found_ref[base : base + 8, :] = real
            found_ref[base + 16 : base + 24, :] = imag
    lane = lax.broadcasted_iota(jnp.int32, (N, N), 1)
    masks = [lane // 32 == slot for slot in range(4)]
    for step in range(9, 16):
        middle[step * PITCH : step * PITCH + 2 * N, :] = jnp.zeros((2 * N, N), f32)
    ytables = [early_table(tables, "y_even"), early_table(tables, "y_odd")]
    for step in range(9):
        packed = None
        for slot in range(4):
            slab = grid[(4 * step + slot) * N : (4 * step + slot + 1) * N, :]
            packed = slab if packed is None else jnp.where(masks[slot], slab, packed)
        lines = halves(packed.T + found_ref[step * N : (step + 1) * N, :])
        for parity in range(2):
            done = dot3(lines, ytables[parity])
            for slot in range(4):
                real, imag = done[slot * 32 : slot * 32 + 16], done[slot * 32 + 16 : slot * 32 + 32]
                base = step * PITCH + parity * N + slot * 16
                middle[base : base + 16, :] = real[:, 0:N] - imag[:, N : 2 * N]
                middle[base + 64 : base + 80, :] = real[:, N : 2 * N] + imag[:, 0:N]
    density = jnp.zeros((N, N), f32)
    response = jnp.zeros((N, N), f32)
    xtable = early_table(tables, "x_inverse")
    for band in range(SUBS):
        sides = []
        for which in range(2):
            rows = []
            for part in range(2):
                for parity in range(2):
                    for slot in range(4):
                        base = parity * N + part * 64 + slot * 16 + band * 2 + which
                        rows.append(middle[pl.ds(base, 16, stride=PITCH), :])
            sides.append(jnp.concatenate(rows, 0))
        field = dot3(xtable, halves(jnp.concatenate(sides, 1)))
        fields_ref[band] = field
        first, second = field[:, 0:N], field[:, N : 2 * N]
        density = density + first[0:N] * first[0:N] + first[N : 2 * N] * first[N : 2 * N]
        response = response + first[0:N] * second[0:N] + first[N : 2 * N] * second[N : 2 * N]
    density = density * (1.0 / BANDS)
    response = response * (2.0 / BANDS)
    spectrum = dot3(
        halves(dot3(early_table(tables, "real"), halves(response))), early_table(tables, "real_turned")
    )
    for half in range(2):
        sums_ref[pl.ds(half, 64, stride=4), :] = density[half * 64 : half * 64 + 64]
        sums_ref[pl.ds(2 + half, 64, stride=4), :] = spectrum[half * 64 : half * 64 + 64]


def mix_kernel(arrived_ref, sums_ref, spread_ref):
    for x_low in range(2):
        base = x_low * 128
        rows = [arrived_ref[base + copy * 32 : base + copy * 32 + 32, :] for copy in range(4)]
        sums_ref[x_low * 32 : x_low * 32 + 32, :] = (rows[0] + rows[1]) + (rows[2] + rows[3])
    spectrum = [sums_ref[pl.ds(2 + half, 16, stride=4), :] for half in range(2)]
    for copy in range(8):
        for half in range(2):
            base = copy * 32 + half * 16
            spread_ref[base : base + 16, :] = spectrum[half]


def hartree_kernel(sums_ref, columns_ref, tables_ref, out_ref):
    sides = []
    for half in range(2):
        sides.append(jnp.concatenate([columns_ref[z * 32 + half * 16 : z * 32 + half * 16 + 16, :] for z in range(8)], 0))
    lines = dot3(late_table(tables_ref, "real_planes"), halves(jnp.concatenate(sides, 1)))
    shape = (N, 2 * N)
    row = lax.broadcasted_iota(jnp.int32, shape, 0)
    lane = lax.broadcasted_iota(jnp.int32, shape, 1)
    across = lax.axis_index(BAND_AXES) * 2 + lax.axis_index("xh") + jnp.where(lane >= N, 64, 0)
    inplane = lane & (N - 1)

    def frequency(index):
        return jnp.where(index <= N // 2, index, index - N // 2)

    across, inplane, row = frequency(across), frequency(inplane), frequency(row)
    squares = (row * row + across * across + inplane * inplane).astype(f32)
    kernel = jnp.where(squares == 0.0, 0.0, (4.0 * math.pi / FACTOR) / jnp.where(squares == 0.0, 1.0, squares))
    back = dot3(late_table(tables_ref, "planes_real"), halves(lines * kernel))
    own = lax.axis_index("z")
    mine = back[0:16]
    for z in range(1, 8):
        mine = jnp.where(own == z, back[z * 16 : z * 16 + 16], mine)
    back = mine
    for half in range(2):
        fields = [
            back[:, half * N : (half + 1) * N],
            sums_ref[pl.ds(half, 16, stride=4), :],
            sums_ref[pl.ds(2 + half, 16, stride=4), :],
        ]
        for which, field in enumerate(fields):
            for x_low in range(2):
                for copy in range(4):
                    base = (x_low * 32 + copy * 8) * 6 + which * 2 + half
                    out_ref[pl.ds(base, 8, stride=6), :] = field[x_low * 8 : x_low * 8 + 8]


def own_plane():
    return lax.axis_index(GA_AXES) * SUBS + lax.axis_index(("xl", "yl", "core"))


def ions_kernel(
    atom_ref,
    direction_ref,
    positions_ref,
    charge_ref,
    widths_ref,
    table_ref,
    potential_ref,
    core_ref,
    early_ref,
    late_ref,
    lines_ref,
    columns_ref,
    out_ref,
    early_out,
    late_out,
    sources_ref,
    centres,
    spreads,
    marks,
    charges,
    arrivals,
):
    del lines_ref
    own = lax.axis_index(("xl", "yl", "core"))
    copies = [
        pltpu.make_async_copy(potential_ref.at[own], out_ref.at[0], arrivals.at[0]),
        pltpu.make_async_copy(core_ref.at[own], out_ref.at[1], arrivals.at[1]),
        pltpu.make_async_copy(early_ref, early_out, arrivals.at[2]),
        pltpu.make_async_copy(late_ref, late_out, arrivals.at[3]),
    ]
    for copy in copies:
        copy.start()
    for slot in range(DISP):
        atom = atom_ref[slot]
        charges[slot : slot + 1, :] = jnp.full((1, N), charge_ref[atom] * (-1.0 / CELL), f32)
        for axis in range(3):
            row = axis * DISP + slot
            centres[row : row + 1, :] = jnp.full((1, N), positions_ref[axis, atom], f32)
            spreads[row : row + 1, :] = jnp.full((1, N), widths_ref[atom], f32)
            marks[row : row + 1, :] = jnp.full((1, N), jnp.where(direction_ref[slot] == axis, 1.0, 0.0), f32)
    frequency = lax.broadcasted_iota(jnp.int32, (3 * DISP, N), 1) - N // 2
    wavenum = frequency.astype(f32) * (2.0 * math.pi / CELL)
    damping = jnp.exp(-0.5 * (wavenum * spreads[...]) ** 2)
    phase = wavenum * centres[...]
    cosine, sine = damping * jnp.cos(phase), damping * jnp.sin(phase)
    chosen = marks[...] > 0.5
    with_cos = jnp.where(chosen, -wavenum * sine, cosine)
    with_sin = jnp.where(chosen, wavenum * cosine, sine)
    profiles = dot3(halves(jnp.concatenate([with_cos, with_sin], 1)), pair(table_ref))
    along_x, along_y, along_z = profiles[0:8], profiles[8:16], profiles[16:24]
    lane = lax.broadcasted_iota(jnp.int32, (DISP, N), 1)
    here = jnp.sum(jnp.where(lane == own_plane(), along_z, 0.0), 1, keepdims=True)
    scaled = along_y * here * charges[...]
    padding = jnp.zeros((N - DISP, N), f32)
    left = jnp.concatenate([along_x, padding], 0).T
    right = jnp.concatenate([scaled, padding], 0)
    out_ref[2] = dot3(halves(left), halves(right))
    place, held, ignored = box_cell(*stick_frequencies(columns_ref[GROUPS : 2 * GROUPS, :]))
    pairs = lax.broadcasted_iota(jnp.int32, (PAIRS, N), 0)
    lanes = lax.broadcasted_iota(jnp.int32, (PAIRS, N), 1).astype(f32)
    places = lax.broadcasted_iota(jnp.int32, (N, N), 0)
    found = jnp.zeros((2 * PAIRS, N), f32)
    for vector in range(GROUPS):
        here = held[vector : vector + 1] == pairs
        marks = jnp.concatenate([jnp.where(here, vector + 1.0, 0.0), jnp.where(here, lanes, 0.0)], 0).astype(bf16)
        spots = jnp.where(place[vector : vector + 1] == places, 1.0, 0.0).astype(bf16)
        found = found + dot(marks, spots, ((1,), (1,)))
    sources_ref[0] = found[0:PAIRS].astype(jnp.int32)
    sources_ref[1] = found[PAIRS : 2 * PAIRS].astype(jnp.int32)
    for copy in copies:
        copy.wait()


def products_kernel(columns_ref, fields_ref, solved_ref, planes_ref, tables_ref, out_ref, lines, cells):
    def solved(which):
        return jnp.concatenate([solved_ref[pl.ds(which * 2 + half, 64, stride=6), :] for half in range(2)], 0)

    waves = dot3(late_table(tables_ref, "real_turned"), halves(jnp.concatenate([solved(0), solved(2)], 1)))
    waves = dot3(halves(jnp.concatenate([waves[:, 0:N], waves[:, N : 2 * N]], 0)), late_table(tables_ref, "real"))
    hartree, response = waves[0:N], waves[N : 2 * N]
    total = solved(1) + planes_ref[1]
    root = jnp.exp(jnp.log(total) * (1.0 / 3.0))
    exchange = -SLATER * root
    effective = planes_ref[0] + exchange
    change = exchange / (3.0 * total) * response + hartree + planes_ref[2]
    xtable = late_table(tables_ref, "x_forward")
    ytable = late_table(tables_ref, "y_forward")
    ytwice = jnp.concatenate([ytable[0], ytable[0]], 0)
    effective2 = jnp.concatenate([effective, effective], 0)
    change2 = jnp.concatenate([change, change], 0)
    lower = lax.broadcasted_iota(jnp.int32, (PAIRS, N), 1) < 64
    for couple in range(SUBS // 2):
        sides = []
        for band in (2 * couple, 2 * couple + 1):
            sides.append(effective2 * fields_ref[band, :, N : 2 * N] + change2 * fields_ref[band, :, 0:N])
        across = dot3(xtable, halves(jnp.concatenate(sides, 1)))
        rows = jnp.concatenate([across[:, 0:N], across[:, N : 2 * N]], 0)
        high, low = halves(rows)
        done = dot(jnp.concatenate([high, low], 1), ytwice) + dot(high, ytable[1])
        for side in range(2):
            real = done[side * 4 * PAIRS : side * 4 * PAIRS + 2 * PAIRS]
            imag = done[side * 4 * PAIRS + 2 * PAIRS : (side + 1) * 4 * PAIRS]
            whole = (real[:, 0:N] + imag[:, N : 2 * N], imag[:, 0:N] - real[:, N : 2 * N])
            for part in range(2):
                base = (part * SUBS + 2 * couple + side) * PAIRS
                lines[base : base + PAIRS, :] = jnp.where(lower, whole[part][0:PAIRS], whole[part][PAIRS : 2 * PAIRS])
    for couple in range(CUT + 1):
        for part in range(2):
            at = (couple * 2 + part) * SUBS
            cells[at : at + SUBS, :] = lines[pl.ds(part * SUBS * PAIRS + couple, SUBS, stride=PAIRS), :]
    across, inplane = stick_frequencies(columns_ref[...])
    place, held, sign = box_cell(across, inplane)
    for vector in range(2 * GROUPS):
        index = jnp.broadcast_to(place[vector : vector + 1], (SUBS, N))
        wanted = jnp.broadcast_to(held[vector : vector + 1], (SUBS, N))
        picked = [jnp.zeros((SUBS, N), f32)] * 2
        for couple in range(CUT + 1):
            mask = wanted == couple
            for part in range(2):
                at = (couple * 2 + part) * SUBS
                found = jnp.take_along_axis(cells[at : at + SUBS, :], index, axis=1)
                picked[part] = jnp.where(mask, found, picked[part])
        picked[1] = picked[1] * sign[vector : vector + 1]
        for part in range(2):
            row = (vector // 2) * 4 + part * 2 + vector % 2
            out_ref[pl.ds(row, SUBS, stride=64), :] = picked[part]


def result_kernel(arrived_ref, tangent_ref, columns_ref, table_ref, out_ref):
    sides = []
    for half in range(2):
        parts = [arrived_ref[pl.ds(part * 2 + half, N, stride=4), :] for part in range(2)]
        sides.append(jnp.concatenate(parts, 0))
    lines = dot3(pair(table_ref), halves(jnp.concatenate(sides, 1)))
    radius = sphere_radius(own_columns(columns_ref))
    inside = radius <= CUT * CUT
    kinetic = (0.5 * FACTOR) * radius.astype(f32)
    for part in range(2):
        kept = jnp.concatenate([tangent_ref[0, part, 0:40, :], tangent_ref[0, part, 96:128, :]], 0)
        rows = jnp.where(inside, lines[part * LINE : (part + 1) * LINE] + kinetic * kept, 0.0)
        out_ref[0, part, 0:40, :] = rows[0:40]
        out_ref[0, part, 40:96, :] = jnp.zeros((56, 256), f32)
        out_ref[0, part, 96:128, :] = rows[40:72]


def vmem(count):
    return [pl.BlockSpec(memory_space=pltpu.VMEM)] * count


def anywhere(count):
    return [pl.BlockSpec(memory_space=pltpu.HBM)] * count


def smem(count):
    return [pl.BlockSpec(memory_space=pltpu.SMEM)] * count


def shape(*dims):
    return jax.ShapeDtypeStruct(dims, f32)


def call(kernel, out_shape, in_specs, mebibytes, scratch=()):
    several = isinstance(out_shape, tuple)
    return pl.pallas_call(
        kernel,
        out_shape=out_shape,
        in_specs=in_specs,
        out_specs=tuple(vmem(len(out_shape))) if several else vmem(1)[0],
        scratch_shapes=scratch,
        compiler_params=pltpu.CompilerParams(vmem_limit_bytes=(mebibytes << 20) or None),
        name=kernel.__name__.removesuffix("_kernel"),
    )


def stay(values):
    return pltpu.with_memory_space_constraint(jnp.asarray(values), pltpu.HBM)


def exchange(values, axes):
    return lax.all_to_all(values, axes, 0, 0, tiled=True)


def body(
    orbitals,
    orbital_tangent,
    stick_columns,
    ion_potential,
    core_density,
    positions,
    z_charge,
    widths,
    atom_index,
    direction,
):
    columns = stick_columns.reshape(STICKS // N, N)
    across, inplane = stick_frequencies(stick_columns)
    place, held, ignored = box_cell(across, inplane)
    dest = jnp.where(held >= 0, held * N + place, DUMP).reshape(GROUPS, 2, N)[:8]
    dest = (dest[:, 0] + dest[:, 1] * 65536).reshape(-1)
    lines = call(lines_kernel, pltpu.VMEM((N * 8, N), f32), vmem(4), 8)(
        stay(orbitals), stay(orbital_tangent), stay(columns), stay(z_inverse_table())
    )
    arrived = exchange(lines.reshape(N, 8, N), PLANE_AXES)
    planes, early, late, sources = call(
        ions_kernel,
        (pltpu.VMEM((3, N, N), f32), pltpu.VMEM(EARLY.shape, bf16), pltpu.VMEM(LATE.shape, bf16), pltpu.VMEM((2, PAIRS, N), jnp.int32)),
        smem(5) + vmem(1) + anywhere(5) + vmem(1),
        8,
        [pltpu.VMEM((24, N), f32)] * 3 + [pltpu.VMEM((8, N), f32), pltpu.SemaphoreType.DMA((4,))],
    )(
        atom_index,
        direction,
        positions.T,
        z_charge,
        widths,
        profile_table(),
        stay(ion_potential),
        stay(core_density),
        stay(EARLY),
        stay(LATE),
        lines,
        columns,
    )
    fields, sums = call(
        fields_kernel,
        (shape(SUBS, 2 * N, 2 * N), shape(2 * N, N)),
        smem(1) + vmem(3),
        20,
        [
            pltpu.VMEM((4, 4 * N, N), f32),
            pltpu.VMEM((CELLS, N), f32),
            pltpu.VMEM((SLABS * 32, N), f32),
            pltpu.VMEM((16 * PITCH, N), f32),
        ],
    )(dest, arrived, early, sources)
    sums = exchange(sums.reshape(64, 4, N), BAND_AXES + ("xh",)).reshape(2 * N, N)
    sums, spectrum = call(mix_kernel, (shape(64, N), shape(2 * N, N)), vmem(1), 4)(sums)
    spectrum = exchange(spectrum.reshape(8, 32, N), "z").reshape(2 * N, N)
    solved = call(hartree_kernel, shape(3 * N, N), vmem(3), 4)(sums, spectrum, late)
    solved = exchange(solved.reshape(64, 3, 2, N), BAND_AXES + ("xh",)).reshape(3 * N, N)
    outgoing = call(products_kernel, shape(4 * N, N), vmem(5), 20, [pltpu.VMEM((16 * PAIRS, N), f32), pltpu.VMEM((66 * SUBS, N), f32)])(
        columns, fields, solved, planes, late
    )
    arrived = exchange(outgoing.reshape(N, 4, N), PLANE_AXES).reshape(4 * N, N)
    return call(result_kernel, shape(1, 2, N, 256), vmem(4), 8)(arrived, orbital_tangent, columns, z_forward_table())


def solution(mesh):
    fine = Mesh(mesh.devices.reshape(2, 4, 2, 2, 2, 8), BAND_AXES + GA_AXES)
    lines = P(BAND_AXES, None, None, GA_AXES)
    planes = P(GA_AXES, None, None)
    return jax.shard_map(
        body,
        mesh=fine,
        in_specs=(lines, lines, P(), planes, planes, P(), P(), P(), P(), P()),
        out_specs=lines,
        check_vma=False,
    )
```
